512 devices in a mesh: row: 16 (over x, y_lo), col: 16 (over z, y_hi), layer: 2 (over core).
Axes of the slice: x: 4, y: 8 (y_hi: 2, y_lo: 4; y = y_hi * 4 + y_lo), z: 8, core: 2. Of those that a mesh axis runs over, the one named last changes fastest.
Arguments:
- ham_blocks: bfloat16 [1472, 11776], P('row', 'col'), may hold values from -0.15625 to 0.15625
- ham_index: int32 [2, 16, 128], P(None, 'row', 'col'), may hold values from 0 to 3
- ham_count: int32 [16, 16], P('row', 'col'), may hold values from 1 to 8, as said below
- dens_blocks: bfloat16 [1472, 11776], P('row', 'col'), may hold values from -6 to 6
- dens_index: int32 [2, 16, 128], P(None, 'row', 'col'), may hold values from 0 to 3
- dens_count: int32 [16, 16], P('row', 'col'), may hold values from 1 to 8, as said below
- first_index: int32 [2, 16, 128], P(None, 'row', 'col'), may hold values from 0 to 3
- first_count: int32 [16, 16], P('row', 'col'), may hold values from 1 to 8, as said below
- second_index: int32 [2, 16, 128], P(None, 'row', 'col'), may hold values from 0 to 3
- second_count: int32 [16, 16], P('row', 'col'), may hold values from 1 to 8, as said below
- third_index: int32 [2, 16, 128], P(None, 'row', 'col'), may hold values from 0 to 3
- third_count: int32 [16, 16], P('row', 'col'), may hold values from 1 to 8, as said below
Outputs:
- real_part: float32 [5888, 5888], P('row', 'col')
- imag_part: float32 [5888, 5888], P('row', 'col')
The draws below stay inside these ranges and needn't reach their ends.
Inputs may be any that keep to these rules, and one draw needn't show every extreme that they name: `ham_count`: in each tile the used slots name distinct blocks; in every draw some tile uses all 8 slots. `dens_count`: in each tile the used slots name distinct blocks; in every draw some tile uses all 8 slots. `first_count`: in each tile the used slots name distinct blocks; in every draw some tile uses all 8 slots. `second_count`: in each tile the used slots name distinct blocks; in every draw some tile uses all 8 slots. `third_count`: in each tile the used slots name distinct blocks; in every draw some tile uses all 8 slots.
All inputs are finite; a program needn't handle non-finite values.
Results may differ from the reference program's by a relative error of at most 0.0003.
Values may be sent and summed in bfloat16 or wider, within the bound.
No kernel may reach another device: no remote copies, remote signals or barrier semaphores. Data moves between devices by JAX's collectives and lax.ppermute only.
A program may use at most 64 MiB of HBM per device.

```python
import jax
import jax.numpy as jnp
from jax import lax

BLK = 92
BT = 4
CAP = 8
NBLK = 64
N_ROW = 16
N_COL = 16


def pattern(key, salt):
    key = jax.random.fold_in(key, salt)
    key_perm, key_shift, key_full = jax.random.split(key, 3)
    tile_total = N_ROW * N_COL
    tile_keys = jax.random.split(key_perm, tile_total)
    orders = jax.vmap(lambda one_key: jax.random.permutation(one_key, BT * BT))(tile_keys)[:, :CAP]
    block_rows = (orders // BT).reshape(N_ROW, N_COL * CAP)
    block_cols = (orders % BT).reshape(N_ROW, N_COL * CAP)
    indices = jnp.stack([block_rows, block_cols]).astype(jnp.int32)
    shifts = jax.random.randint(key_shift, (tile_total,), 0, 4)
    counts = jnp.right_shift(jnp.full((tile_total,), CAP, jnp.int32), shifts.astype(jnp.int32))
    full_tile = jax.random.randint(key_full, (), 0, tile_total)
    counts = jnp.where(jnp.arange(tile_total) == full_tile, CAP, counts)
    return (indices, counts.reshape(N_ROW, N_COL).astype(jnp.int32))


def draw_ham_index(key, part):
    return pattern(key, 11)[0]


def draw_ham_count(key, part):
    return pattern(key, 11)[1]


def draw_dens_index(key, part):
    return pattern(key, 23)[0]


def draw_dens_count(key, part):
    return pattern(key, 23)[1]


def draw_first_index(key, part):
    return pattern(key, 37)[0]


def draw_first_count(key, part):
    return pattern(key, 37)[1]


def draw_second_index(key, part):
    return pattern(key, 41)[0]


def draw_second_count(key, part):
    return pattern(key, 41)[1]


def draw_third_index(key, part):
    return pattern(key, 53)[0]


def draw_third_count(key, part):
    return pattern(key, 53)[1]


def block_scale(rng, shape, pieces, least, top_value):
    loudness = 1.0
    for position, blocks in pieces:
        heights = jax.random.uniform(jax.random.fold_in(jax.random.fold_in(rng, 6), position), (blocks,), jnp.float32, least / len(pieces), top_value / len(pieces))
        loudness = loudness * jnp.repeat(jnp.exp(heights), shape[position] // blocks).reshape((-1,) + (1,) * (len(shape) - 1 - position))
    return loudness


def normal_values(stream_key, shape, deviation, bound, cuts=(), dtype=jnp.bfloat16):
    drawn = deviation * jax.random.normal(stream_key, shape, jnp.float32)
    if cuts:
        drawn = drawn * block_scale(stream_key, shape, cuts, -0.22, 0.18)
    return jnp.clip(drawn, -bound, bound).astype(dtype)


def setup_inputs(seed: int = 0) -> dict:
    arg_keys = jax.random.split(jax.random.key(seed), 13)
    ham_blocks = normal_values(arg_keys[0], (N_ROW * BLK, N_COL * CAP * BLK), (NBLK * BLK // 4) ** -0.5, 0.15625, ((0, 16), (1, 16)))
    ham_index = draw_ham_index(jax.random.fold_in(arg_keys[12], 71), 0)
    ham_count = draw_ham_count(jax.random.fold_in(arg_keys[12], 71), 0)
    dens_blocks = normal_values(arg_keys[3], (N_ROW * BLK, N_COL * CAP * BLK), 1.0, 6.0, ((0, 16), (1, 16)))
    dens_index = draw_dens_index(jax.random.fold_in(arg_keys[12], 71), 0)
    dens_count = draw_dens_count(jax.random.fold_in(arg_keys[12], 71), 0)
    first_index = draw_first_index(jax.random.fold_in(arg_keys[12], 71), 0)
    first_count = draw_first_count(jax.random.fold_in(arg_keys[12], 71), 0)
    second_index = draw_second_index(jax.random.fold_in(arg_keys[12], 71), 0)
    second_count = draw_second_count(jax.random.fold_in(arg_keys[12], 71), 0)
    third_index = draw_third_index(jax.random.fold_in(arg_keys[12], 71), 0)
    third_count = draw_third_count(jax.random.fold_in(arg_keys[12], 71), 0)
    return {"ham_blocks": ham_blocks, "ham_index": ham_index, "ham_count": ham_count, "dens_blocks": dens_blocks, "dens_index": dens_index, "dens_count": dens_count, "first_index": first_index, "first_count": first_count, "second_index": second_index, "second_count": second_count, "third_index": third_index, "third_count": third_count}


def selectors(index, count):
    slot_ids = jnp.arange(CAP)
    in_use = slot_ids[None, None, :] < count[:, :, None]
    indices = index.reshape(2, N_ROW, N_COL, CAP)
    positions = jnp.arange(BT)
    row_pick = (indices[0][..., None] == positions) & in_use[..., None]
    col_pick = (indices[1][..., None] == positions) & in_use[..., None]
    return (row_pick[..., :, None] & col_pick[..., None, :]).astype(jnp.float32)


def dense_matrix(blocks, index, count):
    chosen = selectors(index, count)
    stacked = blocks.astype(jnp.float32).reshape(N_ROW, BLK, N_COL, CAP, BLK)
    whole = jnp.einsum("rcsij,racsb->riacjb", chosen, stacked)
    return whole.reshape(N_ROW * BT * BLK, N_COL * BT * BLK)


def block_mask(index, count):
    chosen = selectors(index, count).sum(axis=2)
    coarse = jnp.transpose(chosen, (0, 2, 1, 3)).reshape(N_ROW * BT, N_COL * BT)
    return jnp.repeat(jnp.repeat(coarse, BLK, axis=0), BLK, axis=1)


def to_bf16(values):
    rounded = values.astype(jnp.bfloat16)
    rounded = lax.optimization_barrier(rounded)
    return rounded.astype(jnp.float32)


def reference(ham_blocks, ham_index, ham_count, dens_blocks, dens_index, dens_count, first_index, first_count, second_index, second_count, third_index, third_count):
    ham = dense_matrix(ham_blocks, ham_index, ham_count)
    dens = dense_matrix(dens_blocks, dens_index, dens_count)

    def apply_ham(right):
        return jnp.dot(ham, right, precision=lax.Precision.HIGHEST, preferred_element_type=jnp.float32)

    first_term = block_mask(first_index, first_count) * apply_ham(dens)
    second_term = block_mask(second_index, second_count) * apply_ham(to_bf16(first_term))
    third_term = block_mask(third_index, third_count) * apply_ham(to_bf16(second_term))
    real_part = dens - 0.5 * second_term
    imag_part = third_term / 6.0 - first_term
    return real_part, imag_part
```

```python
import functools

import jax
import jax.numpy as jnp
from jax import lax
from jax.experimental import pallas as pl
from jax.experimental.pallas import tpu as pltpu
from jax.sharding import Mesh, PartitionSpec as P

BLK = 92
HALF = 46
BT = 4
CAP = 8
ROWS = 96
COLS = 48
LANES = 128
SIDE = BT * BLK
WIRE = 768
META = 736
TILES = 16
BF = jnp.bfloat16
F32 = jnp.float32
VMEM = pl.BlockSpec(memory_space=pltpu.VMEM)
SMEM = pl.BlockSpec(memory_space=pltpu.SMEM)
PARAMS = pltpu.CompilerParams(vmem_limit_bytes=48 * 1024 * 1024)


def dot_nt(a, b):
    return lax.dot_general(a, b, (((1,), (1,)), ((), ())), preferred_element_type=F32)


def one_hot(shape, shift, width):
    q = lax.broadcasted_iota(jnp.int32, shape, 0)
    x = lax.broadcasted_iota(jnp.int32, shape, 1)
    return jnp.where((x == q + shift) & (q < width), 1.0, 0.0).astype(BF)


def prep_kernel(layer_ref, code_ref, ham_ref, dens_ref, hmeta_ref, dmeta_ref,
                hwire_ref, dwire_ref, dense_ref, pad_ref):
    layer = layer_ref[0]
    lane = lax.broadcasted_iota(jnp.int32, (COLS, LANES), 1)
    pad_ref[...] = jnp.zeros_like(pad_ref)
    pad_ref[0:BLK, 0:META] = ham_ref[...]
    start = pl.multiple_of(layer * COLS, 16)
    hwire_ref[...] = pad_ref[pl.ds(start, COLS), :]
    last = hwire_ref[:, WIRE - LANES:]
    hwire_ref[:, WIRE - LANES:] = jnp.where(lane >= META - (WIRE - LANES), hmeta_ref[...], last)
    dens = dens_ref[...]
    dense_ref[...] = jnp.zeros_like(dense_ref)
    pieces = []
    for s in range(CAP):
        pick = one_hot((COLS, META), s * BLK + layer * HALF, HALF)
        piece = dot_nt(pick, dens)
        pieces.append(piece.astype(BF))
        code = code_ref[0, s]
        at = jnp.maximum(code, 0)
        i, j = at // BT, at % BT
        x = lax.broadcasted_iota(jnp.int32, (META, BT * COLS), 0)
        y = lax.broadcasted_iota(jnp.int32, (META, BT * COLS), 1) - j * COLS
        spread = jnp.where(
            (x == y + (s * BLK + layer * HALF)) & (y >= 0) & (y < HALF) & (code >= 0), 1.0, 0.0
        ).astype(BF)
        block = jnp.dot(dens, spread, preferred_element_type=F32)
        block = jnp.concatenate([block, jnp.zeros((ROWS - BLK, BT * COLS), F32)], axis=0)
        rows = pl.ds(pl.multiple_of(i * ROWS, ROWS), ROWS)
        dense_ref[rows, :] = dense_ref[rows, :] + block
    pieces.append(jnp.zeros((COLS, WIRE - META), BF))
    wire = jnp.concatenate(pieces, axis=1)
    tail = jnp.where(lane >= META - (WIRE - LANES), dmeta_ref[...], wire[:, WIRE - LANES:])
    dwire_ref[0, :, 0:WIRE - LANES] = wire[:, 0:WIRE - LANES]
    dwire_ref[0, :, WIRE - LANES:] = tail
    for n in range(1, TILES):
        dwire_ref[n] = dwire_ref[0]


def ham_kernel(layer_ref, code_ref, own_ref, other_ref, out_ref):
    layer = layer_ref[0]
    out_ref[...] = jnp.zeros_like(out_ref)

    def tile(k, carry):
        for ref, part in ((own_ref, layer), (other_ref, 1 - layer)):
            wire = ref[k]
            for s in range(CAP):
                code = code_ref[k, s]
                at = jnp.maximum(code, 0)
                where = jnp.where(code >= 0, k, TILES)
                rows = pl.ds(pl.multiple_of((at // BT) * ROWS + part * COLS, 16), COLS)
                lanes = pl.ds(pl.multiple_of((at % BT) * LANES, LANES), BLK)
                out_ref[where, rows, lanes] = wire[:, s * BLK:(s + 1) * BLK]
        return carry

    lax.fori_loop(0, TILES, tile, 0)


def product(ham_ref, code_ref, wire_ref, right_ref):
    right_ref[...] = jnp.zeros_like(right_ref)

    def tile(k, carry):
        wire = wire_ref[k]
        for s in range(CAP):
            code = code_ref[k, s]
            at = jnp.maximum(code, 0)
            where = jnp.where(code >= 0, k, TILES)
            rows = pl.ds(pl.multiple_of((at % BT) * COLS, 16), COLS)
            lanes = pl.ds(pl.multiple_of((at // BT) * LANES, LANES), BLK)
            right_ref[where, rows, lanes] = wire[:, s * BLK:(s + 1) * BLK]
        return carry

    lax.fori_loop(0, TILES, tile, 0)
    total = jnp.zeros((BT * ROWS, BT * COLS), F32)

    def add(k, total):
        return total + dot_nt(ham_ref[k], right_ref[k])

    return lax.fori_loop(0, TILES, add, total)


def keep(code_ref, total):
    row = lax.broadcasted_iota(jnp.int32, total.shape, 0) // ROWS
    col = lax.broadcasted_iota(jnp.int32, total.shape, 1) // COLS
    place = row * BT + col
    kept = place == code_ref[0, 0]
    for s in range(1, CAP):
        kept = kept | (place == code_ref[0, s])
    return jnp.where(kept, total, 0.0)


def pack(code_ref, term, rounded_ref, wire_ref):
    rounded_ref[...] = term.astype(BF)
    pieces = []
    for s in range(CAP):
        at = jnp.maximum(code_ref[0, s], 0)
        pick = one_hot((COLS, BT * COLS), (at % BT) * COLS, COLS)
        rows = pl.ds(pl.multiple_of((at // BT) * ROWS, 16), ROWS)
        pieces.append(dot_nt(pick, rounded_ref[rows, :]).astype(BF)[:, 0:BLK])
    pieces.append(jnp.zeros((COLS, WIRE - META), BF))
    wire = jnp.concatenate(pieces, axis=1)
    for n in range(TILES):
        wire_ref[n] = wire


def first_kernel(code_ref, keep_ref, ham_ref, wire_ref, term_ref, out_ref, right_ref, rounded_ref):
    term = keep(keep_ref, product(ham_ref, code_ref, wire_ref, right_ref))
    term_ref[...] = term
    pack(keep_ref, term, rounded_ref, out_ref)


def second_kernel(code_ref, keep_ref, ham_ref, wire_ref, dense_ref, real_ref, out_ref, right_ref,
                  rounded_ref):
    term = keep(keep_ref, product(ham_ref, code_ref, wire_ref, right_ref))
    real_ref[...] = dense_ref[...] - 0.5 * term
    pack(keep_ref, term, rounded_ref, out_ref)


def third_kernel(code_ref, keep_ref, ham_ref, wire_ref, first_ref, imag_ref, right_ref):
    term = keep(keep_ref, product(ham_ref, code_ref, wire_ref, right_ref))
    imag_ref[...] = term / 6.0 - first_ref[...]


def join_kernel(layer_ref, own_ref, other_ref, out_ref):
    swap = layer_ref[0] == 1
    own, other = own_ref[...], other_ref[...]
    low, high = jnp.where(swap, other, own), jnp.where(swap, own, other)
    pieces = []
    for j in range(BT):
        pieces += [low[:, j * COLS:j * COLS + HALF], high[:, j * COLS:j * COLS + HALF]]
    whole = jnp.concatenate(pieces, axis=1)
    for i in range(BT):
        out_ref[i * BLK:(i + 1) * BLK, :] = whole[i * ROWS:i * ROWS + BLK, :]


def call(kernel, scalars, arrays, out_shape, scratch=()):
    return pl.pallas_call(
        kernel,
        out_shape=out_shape,
        in_specs=[SMEM] * len(scalars) + [VMEM] * len(arrays),
        out_specs=jax.tree.map(lambda _: VMEM, out_shape),
        scratch_shapes=list(scratch),
        compiler_params=PARAMS,
    )(*scalars, *arrays)


def shape(*dims, dtype=BF):
    return jax.ShapeDtypeStruct(dims, dtype)


def codes(index, count):
    slot = jnp.arange(CAP)
    return jnp.where(slot < count[0, 0], index[0, 0] * BT + index[1, 0], -1)[None, :]


def wire_meta(*lists):
    flat = jnp.concatenate([one[0] for one in lists]).astype(BF)
    flat = jnp.pad(flat, (LANES - (WIRE - META), WIRE - META - flat.shape[0]))
    return jnp.broadcast_to(flat[None, :], (COLS, LANES))


def read_meta(wires, which):
    return wires[:, 0, META + which * CAP:META + (which + 1) * CAP].astype(jnp.int32)


def swap(values, axis):
    return lax.ppermute(values, axis, [(0, 1), (1, 0)])


def per_device(ham_blocks, ham_index, ham_count, dens_blocks, dens_index, dens_count, first_index,
               first_count, second_index, second_count, third_index, third_count):
    layer = lax.axis_index("layer").astype(jnp.int32).reshape(1)
    ham_code = codes(ham_index, ham_count)
    dens_code = codes(dens_index, dens_count)
    first_code = codes(first_index, first_count)
    second_code = codes(second_index, second_count)
    third_code = codes(third_index, third_count)
    ham_wire, dens_wire, dens_half = call(
        prep_kernel,
        (layer, dens_code),
        (ham_blocks, dens_blocks, wire_meta(ham_code), wire_meta(dens_code, first_code, second_code)),
        (shape(COLS, WIRE), shape(TILES, COLS, WIRE), shape(BT * ROWS, BT * COLS, dtype=F32)),
        [pltpu.VMEM((ROWS, WIRE), BF)],
    )
    far = swap(ham_wire, "y_hi")
    y_hi = lax.axis_index("y_hi")
    pair = jnp.where(y_hi == 0, jnp.stack([ham_wire, far]), jnp.stack([far, ham_wire]))
    depth = lax.axis_size("z")
    panel = lax.all_to_all(jnp.broadcast_to(pair, (depth,) + pair.shape), "z", 0, 0)
    panel = panel.reshape(TILES, COLS, WIRE)
    other = swap(panel, "layer")

    def gather(wires):
        return lax.all_to_all(wires, ("x", "y_lo"), 0, 0)

    right = gather(dens_wire)
    in_dens, in_first, in_second = (read_meta(right, n) for n in range(3))
    ham = call(
        ham_kernel, (layer, read_meta(panel, 0)), (panel, other),
        shape(TILES + 1, BT * ROWS, BT * LANES),
    )
    half = shape(BT * ROWS, BT * COLS, dtype=F32)
    dense_right = pltpu.VMEM((TILES + 1, BT * COLS, BT * LANES), BF)
    rounded = pltpu.VMEM((BT * ROWS, BT * COLS), BF)
    wires = shape(TILES, COLS, WIRE)
    first_term, first_wire = call(
        first_kernel, (in_dens, first_code), (ham, right), (half, wires), [dense_right, rounded]
    )
    real_half, second_wire = call(
        second_kernel, (in_first, second_code), (ham, gather(first_wire), dens_half), (half, wires),
        [dense_right, rounded],
    )
    imag_half = call(
        third_kernel, (in_second, third_code), (ham, gather(second_wire), first_term), half,
        [dense_right],
    )

    def join(part):
        return call(join_kernel, (layer,), (part, swap(part, "layer")), shape(SIDE, SIDE, dtype=F32))

    return join(real_half), join(imag_half)


def solution(mesh):
    axes = ("x", "y_lo", "z", "y_hi", "layer")
    split = Mesh(mesh.devices.reshape(4, 4, 8, 2, 2), axes)
    row, col = ("x", "y_lo"), ("z", "y_hi")
    blocks, index = P(row, col), P(None, row, col)
    in_specs = (blocks, index, blocks) * 2 + (index, blocks) * 3
    return jax.shard_map(
        per_device, mesh=split, in_specs=in_specs, out_specs=(blocks, blocks), check_vma=False
    )
```

```python
import itertools

import jax
import jax.numpy as jnp
from jax import lax
from jax.experimental import pallas as pl
from jax.experimental.pallas import tpu as pltpu
from jax.sharding import Mesh, PartitionSpec as P

BLK = 92
HALF = 46
BT = 4
CAP = 8
ROWS = 96
COLS = 48
LANES = 128
SIDE = BT * BLK
WIRE = 768
META = 736
TILES = 16
AXES = ("x", "y_lo", "z", "y_hi", "layer")
BF = jnp.bfloat16
F32 = jnp.float32
VMEM = pl.BlockSpec(memory_space=pltpu.VMEM)
SMEM = pl.BlockSpec(memory_space=pltpu.SMEM)
PARAMS = pltpu.CompilerParams(vmem_limit_bytes=16 * 1024 * 1024)


def dot_nt(a, b):
    return lax.dot_general(a, b, (((1,), (1,)), ((), ())), preferred_element_type=F32)


def one_hot(shape, shift, width):
    q = lax.broadcasted_iota(jnp.int32, shape, 0)
    x = lax.broadcasted_iota(jnp.int32, shape, 1)
    return jnp.where((x == q + shift) & (q < width), 1.0, 0.0).astype(BF)


def code_of(index_ref, count_ref, s):
    return jnp.where(s < count_ref[0, 0], index_ref[0, 0, s] * BT + index_ref[1, 0, s], -1)


def prep_kernel(hidx_ref, hcnt_ref, didx_ref, dcnt_ref, fidx_ref, fcnt_ref, sidx_ref, scnt_ref,
                ham_ref, dens_ref, out_ref):
    layer = lax.axis_index("layer")
    lane = lax.broadcasted_iota(jnp.int32, (ROWS, LANES), 1) - (META - (WIRE - LANES))

    def noted(tail, *lists):
        for n, (index_ref, count_ref) in enumerate(lists):
            for s in range(CAP):
                code = code_of(index_ref, count_ref, s).astype(F32)
                tail = jnp.where(lane == n * CAP + s, code, tail)
        return tail.astype(BF)

    @pl.when(layer == 0)
    def _():
        dens = dens_ref[...]
        r = lax.broadcasted_iota(jnp.int32, (2 * COLS, META), 0)
        x = lax.broadcasted_iota(jnp.int32, (2 * COLS, META), 1)
        q = r % COLS
        pieces = []
        for s in range(CAP):
            pick = (x == q + (r // COLS) * HALF + s * BLK) & (q < HALF)
            pieces.append(dot_nt(jnp.where(pick, 1.0, 0.0).astype(BF), dens))
        pieces.append(jnp.zeros((2 * COLS, WIRE - META), F32))
        wire = jnp.concatenate(pieces, axis=1)
        out_ref[:, 0:WIRE - LANES] = wire[:, 0:WIRE - LANES].astype(BF)
        out_ref[:, WIRE - LANES:] = noted(
            wire[:, WIRE - LANES:], (didx_ref, dcnt_ref), (fidx_ref, fcnt_ref), (sidx_ref, scnt_ref)
        )

    @pl.when(layer == 1)
    def _():
        out_ref[...] = jnp.zeros_like(out_ref)
        out_ref[0:BLK, 0:META] = ham_ref[...]
        tail = out_ref[:, WIRE - LANES:].astype(F32)
        out_ref[:, WIRE - LANES:] = noted(tail, (hidx_ref, hcnt_ref))


def dense_kernel(didx_ref, dcnt_ref, dens_ref, dense_ref):
    layer = lax.axis_index("layer")
    dens = dens_ref[...]
    dense_ref[...] = jnp.zeros_like(dense_ref)
    for s in range(CAP):
        code = code_of(didx_ref, dcnt_ref, s)
        at = jnp.maximum(code, 0)
        i, j = at // BT, at % BT
        x = lax.broadcasted_iota(jnp.int32, (META, BT * COLS), 0)
        y = lax.broadcasted_iota(jnp.int32, (META, BT * COLS), 1) - j * COLS
        spread = jnp.where(
            (x == y + (s * BLK + layer * HALF)) & (y >= 0) & (y < HALF) & (code >= 0), 1.0, 0.0
        ).astype(BF)
        block = jnp.dot(dens, spread, preferred_element_type=F32)
        block = jnp.concatenate([block, jnp.zeros((ROWS - BLK, BT * COLS), F32)], axis=0)
        rows = pl.ds(pl.multiple_of(i * ROWS, ROWS), ROWS)
        dense_ref[rows, :] = dense_ref[rows, :] + block


def ham_kernel(code_ref, own_ref, other_ref, out_ref):
    layer = lax.axis_index("layer")
    out_ref[...] = jnp.zeros_like(out_ref)

    def unpack(from_ref):
        def tile(k, carry):
            wire = from_ref[k]
            for s in range(CAP):
                code = code_ref[k, s]
                at = jnp.maximum(code, 0)
                where = jnp.where(code >= 0, k, TILES)
                rows = pl.ds(pl.multiple_of((at // BT) * ROWS, 16), ROWS)
                lanes = pl.ds(pl.multiple_of((at % BT) * LANES, LANES), BLK)
                out_ref[where, rows, lanes] = wire[:, s * BLK:(s + 1) * BLK]
            return carry

        lax.fori_loop(0, TILES, tile, 0)

    pl.when(layer == 1)(lambda: unpack(own_ref))
    pl.when(layer == 0)(lambda: unpack(other_ref))


def unpack_right(code_ref, wire_ref, right_ref, first_row):
    def tile(k, carry):
        wire = wire_ref[k, pl.ds(first_row, COLS), :]
        row = k // 4 * 4 + k % 2 * 2 + k // 2 % 2
        for s in range(CAP):
            code = code_ref[k, s]
            at = jnp.maximum(code, 0)
            where = jnp.where(code >= 0, row, TILES)
            rows = pl.ds(pl.multiple_of((at % BT) * COLS, 16), COLS)
            lanes = pl.ds(pl.multiple_of((at // BT) * LANES, LANES), BLK)
            right_ref[where, rows, lanes] = wire[:, s * BLK:(s + 1) * BLK]
        return carry

    lax.fori_loop(0, TILES, tile, 0)


def multiply(ham_ref, right_ref):
    def add(n, total):
        for k in range(BT):
            total = total + dot_nt(ham_ref[n * BT + k], right_ref[n * BT + k])
        return total

    return lax.fori_loop(0, TILES // BT, add, jnp.zeros((BT * ROWS, BT * COLS), F32))


def product(ham_ref, code_ref, wire_ref, right_ref):
    right_ref[...] = jnp.zeros_like(right_ref)
    unpack_right(code_ref, wire_ref, right_ref, 0)
    return multiply(ham_ref, right_ref)


def keep(codes, total):
    row = lax.broadcasted_iota(jnp.int32, total.shape, 0) // ROWS
    col = lax.broadcasted_iota(jnp.int32, total.shape, 1) // COLS
    place = row * BT + col
    kept = place == codes[0]
    for s in range(1, CAP):
        kept = kept | (place == codes[s])
    return jnp.where(kept, total, 0.0)


def pack(codes, term, rounded_ref, wire_ref):
    rounded_ref[...] = term.astype(BF)
    pieces = []
    for s in range(CAP):
        at = jnp.maximum(codes[s], 0)
        pick = one_hot((COLS, BT * COLS), (at % BT) * COLS, COLS)
        rows = pl.ds(pl.multiple_of((at // BT) * ROWS, 16), ROWS)
        pieces.append(dot_nt(pick, rounded_ref[rows, :]).astype(BF)[:, 0:BLK])
    pieces.append(jnp.zeros((COLS, WIRE - META), BF))
    wire_ref[...] = jnp.concatenate(pieces, axis=1)


def all_codes(index_ref, count_ref):
    return [code_of(index_ref, count_ref, s) for s in range(CAP)]


def first_kernel(code_ref, index_ref, count_ref, ham_ref, own_ref, other_ref, term_ref, out_ref,
                 right_ref, rounded_ref):
    layer = lax.axis_index("layer")
    right_ref[...] = jnp.zeros_like(right_ref)
    pl.when(layer == 0)(lambda: unpack_right(code_ref, own_ref, right_ref, 0))
    pl.when(layer == 1)(lambda: unpack_right(code_ref, other_ref, right_ref, COLS))
    codes = all_codes(index_ref, count_ref)
    term = keep(codes, multiply(ham_ref, right_ref))
    term_ref[...] = term
    pack(codes, term, rounded_ref, out_ref)


def second_kernel(code_ref, index_ref, count_ref, ham_ref, wire_ref, dense_ref, real_ref, out_ref,
                  right_ref, rounded_ref):
    codes = all_codes(index_ref, count_ref)
    term = keep(codes, product(ham_ref, code_ref, wire_ref, right_ref))
    real_ref[...] = dense_ref[...] - 0.5 * term
    pack(codes, term, rounded_ref, out_ref)


def third_kernel(code_ref, index_ref, count_ref, ham_ref, wire_ref, first_ref, imag_ref, right_ref):
    codes = all_codes(index_ref, count_ref)
    term = keep(codes, product(ham_ref, code_ref, wire_ref, right_ref))
    imag_ref[...] = term / 6.0 - first_ref[...]


def join_kernel(own_ref, other_ref, out_ref):
    swap = lax.axis_index("layer") == 1
    own, other = own_ref[...], other_ref[...]
    low, high = jnp.where(swap, other, own), jnp.where(swap, own, other)
    pieces = []
    for j in range(BT):
        pieces += [low[:, j * COLS:j * COLS + HALF], high[:, j * COLS:j * COLS + HALF]]
    whole = jnp.concatenate(pieces, axis=1)
    for i in range(BT):
        out_ref[i * BLK:(i + 1) * BLK, :] = whole[i * ROWS:i * ROWS + BLK, :]


def call(kernel, scalars, arrays, out_shape, scratch=()):
    return pl.pallas_call(
        kernel,
        out_shape=out_shape,
        in_specs=[SMEM] * len(scalars) + [VMEM] * len(arrays),
        out_specs=jax.tree.map(lambda _: VMEM, out_shape),
        scratch_shapes=list(scratch),
        compiler_params=PARAMS,
    )(*scalars, *arrays)


def shape(*dims, dtype=BF):
    return jax.ShapeDtypeStruct(dims, dtype)


def place(x, y_lo, z, y_hi, layer):
    return (((x * 4 + y_lo) * 8 + z) * 2 + y_hi) * 2 + layer


def everywhere():
    return list(itertools.product(range(4), range(4), range(8), range(2), range(2)))


def pair_route(both):
    route = []
    for x, y_lo, z, y_hi, layer in everywhere():
        to = (x, y_lo, z, 1 - y_hi, layer) if both and layer else (x, y_lo ^ 2, z, y_hi, layer)
        route.append((place(x, y_lo, z, y_hi, layer), place(*to)))
    return route


def groups(both):
    found = {}
    for x, y_lo, z, y_hi, layer in everywhere():
        key = (layer, x, y_lo, y_hi) if both and layer else (layer, y_lo // 2, z, y_hi)
        found.setdefault(key, []).append(place(x, y_lo, z, y_hi, layer))
    return sorted(found.values())


def gather(piece, first, both):
    far = lax.ppermute(piece, AXES, pair_route(both))
    pair = jnp.where(first, jnp.stack([piece, far]), jnp.stack([far, piece]))
    return lax.all_to_all(
        jnp.broadcast_to(pair, (8,) + pair.shape), AXES, 0, 0, axis_index_groups=groups(both)
    )


def swap(values):
    return lax.ppermute(values, "layer", [(0, 1), (1, 0)])


def per_device(ham_blocks, ham_index, ham_count, dens_blocks, dens_index, dens_count, first_index,
               first_count, second_index, second_count, third_index, third_count):
    layer = lax.axis_index("layer")
    y_first = lax.axis_index("y_lo") < 2
    payload = call(
        prep_kernel,
        (ham_index, ham_count, dens_index, dens_count, first_index, first_count, second_index,
         second_count),
        (ham_blocks, dens_blocks),
        shape(ROWS, WIRE),
    )
    first = jnp.where(layer == 0, y_first, lax.axis_index("y_hi") == 0)
    panel = gather(payload, first, True)
    panel = panel.reshape((TILES,) + panel.shape[2:])
    other = swap(panel)
    notes = jnp.stack([panel[:, 0, META:], other[:, 0, META:]])
    ham_note = notes[1 - layer].astype(jnp.int32)
    dens_note = notes[layer].astype(jnp.int32)
    ham = call(
        ham_kernel, (ham_note[:, 0:CAP],), (panel, other), shape(TILES + 1, BT * ROWS, BT * LANES)
    )
    half = shape(BT * ROWS, BT * COLS, dtype=F32)
    dense_half = call(dense_kernel, (dens_index, dens_count), (dens_blocks,), half)
    dense_right = pltpu.VMEM((TILES + 1, BT * COLS, BT * LANES), BF)
    rounded = pltpu.VMEM((BT * ROWS, BT * COLS), BF)
    wire = shape(COLS, WIRE)

    def codes(which):
        return dens_note[:, which * CAP:(which + 1) * CAP]

    def gathered(piece):
        tiles = gather(piece, y_first, False)
        return tiles.reshape((TILES,) + tiles.shape[2:])

    first_term, first_wire = call(
        first_kernel, (codes(0), first_index, first_count), (ham, panel, other), (half, wire),
        [dense_right, rounded],
    )
    real_half, second_wire = call(
        second_kernel, (codes(1), second_index, second_count),
        (ham, gathered(first_wire), dense_half), (half, wire), [dense_right, rounded],
    )
    imag_half = call(
        third_kernel, (codes(2), third_index, third_count),
        (ham, gathered(second_wire), first_term), half, [dense_right],
    )

    def join(part):
        return call(join_kernel, (), (part, swap(part)), shape(SIDE, SIDE, dtype=F32))

    return join(real_half), join(imag_half)


def solution(mesh):
    split = Mesh(mesh.devices.reshape(4, 4, 8, 2, 2), AXES)
    row, col = ("x", "y_lo"), ("z", "y_hi")
    blocks, index = P(row, col), P(None, row, col)
    in_specs = (blocks, index, blocks) * 2 + (index, blocks) * 3
    return jax.shard_map(
        per_device, mesh=split, in_specs=in_specs, out_specs=(blocks, blocks), check_vma=False
    )
```

```python
import itertools

import jax
import jax.numpy as jnp
from jax import lax
from jax.experimental import pallas as pl
from jax.experimental.pallas import tpu as pltpu
from jax.sharding import Mesh, PartitionSpec as P

BLK = 92
HALF = 46
BT = 4
CAP = 8
ROWS = 96
COLS = 48
LANES = 128
SIDE = BT * BLK
WIRE = 768
META = 736
TAIL = WIRE - LANES
TILES = 16
AXES = ("x", "y_lo", "z", "y_hi", "layer")
BF = jnp.bfloat16
F32 = jnp.float32
VMEM = pl.BlockSpec(memory_space=pltpu.VMEM)
SMEM = pl.BlockSpec(memory_space=pltpu.SMEM)
HBM = pl.BlockSpec(memory_space=pltpu.HBM)


def dot_nt(a, b):
    return lax.dot_general(a, b, (((1,), (1,)), ((), ())), preferred_element_type=F32)


def one_hot(shape, shift, width):
    q = lax.broadcasted_iota(jnp.int32, shape, 0)
    x = lax.broadcasted_iota(jnp.int32, shape, 1)
    return jnp.where((x == q + shift) & (q < width), 1.0, 0.0).astype(BF)


def code_of(index_ref, count_ref, s):
    return jnp.where(s < count_ref[0, 0], index_ref[0, 0, s] * BT + index_ref[1, 0, s], -1)


def prep_kernel(hidx_hbm, hcnt_ref, didx_hbm, dcnt_ref, fidx_hbm, fcnt_ref, sidx_hbm, scnt_ref,
                ham_hbm, dens_hbm, out_ref, hidx_ref, didx_ref, fidx_ref, sidx_ref, ham_ref,
                dens_ref, sems):
    pairs = ((ham_hbm, ham_ref), (dens_hbm, dens_ref), (hidx_hbm, hidx_ref), (didx_hbm, didx_ref),
             (fidx_hbm, fidx_ref), (sidx_hbm, sidx_ref))
    copies = [pltpu.make_async_copy(src, dst, sems.at[n]) for n, (src, dst) in enumerate(pairs)]
    for one in copies:
        one.start()
    for one in copies:
        one.wait()
    layer = lax.axis_index("layer")
    lane = lax.broadcasted_iota(jnp.int32, (ROWS, LANES), 1) - (META - TAIL)

    def noted(tail, *lists):
        for n, (index_ref, count_ref) in enumerate(lists):
            for s in range(CAP):
                code = code_of(index_ref, count_ref, s).astype(F32)
                tail = jnp.where(lane == n * CAP + s, code, tail)
        return tail.astype(BF)

    @pl.when(layer == 0)
    def _():
        dens = dens_ref[...]
        r = lax.broadcasted_iota(jnp.int32, (2 * COLS, META), 0)
        x = lax.broadcasted_iota(jnp.int32, (2 * COLS, META), 1)
        q = r % COLS
        pieces = []
        for s in range(CAP):
            pick = (x == q + (r // COLS) * HALF + s * BLK) & (q < HALF)
            pieces.append(dot_nt(jnp.where(pick, 1.0, 0.0).astype(BF), dens))
        pieces.append(jnp.zeros((2 * COLS, WIRE - META), F32))
        wire = jnp.concatenate(pieces, axis=1)
        out_ref[:, 0:TAIL] = wire[:, 0:TAIL].astype(BF)
        out_ref[:, TAIL:] = noted(
            wire[:, TAIL:], (didx_ref, dcnt_ref), (fidx_ref, fcnt_ref), (sidx_ref, scnt_ref)
        )

    @pl.when(layer == 1)
    def _():
        out_ref[...] = jnp.zeros_like(out_ref)
        out_ref[0:BLK, 0:META] = ham_ref[...]
        tail = out_ref[:, TAIL:].astype(F32)
        out_ref[:, TAIL:] = noted(tail, (hidx_ref, hcnt_ref))


def dense_kernel(didx_ref, dcnt_ref, dens_ref, dense_ref):
    layer = lax.axis_index("layer")
    dens = dens_ref[...]
    dense_ref[...] = jnp.zeros_like(dense_ref)
    for s in range(CAP):
        code = code_of(didx_ref, dcnt_ref, s)
        at = jnp.maximum(code, 0)
        i, j = at // BT, at % BT
        x = lax.broadcasted_iota(jnp.int32, (META, BT * COLS), 0)
        y = lax.broadcasted_iota(jnp.int32, (META, BT * COLS), 1) - j * COLS
        spread = jnp.where(
            (x == y + (s * BLK + layer * HALF)) & (y >= 0) & (y < HALF) & (code >= 0), 1.0, 0.0
        ).astype(BF)
        block = jnp.dot(dens, spread, preferred_element_type=F32)
        block = jnp.concatenate([block, jnp.zeros((ROWS - BLK, BT * COLS), F32)], axis=0)
        rows = pl.ds(pl.multiple_of(i * ROWS, ROWS), ROWS)
        dense_ref[rows, :] = dense_ref[rows, :] + block


def unpack_ham(code_ref, from_ref, out_ref):
    def tile(k, carry):
        wire = from_ref[k]
        for s in range(CAP):
            code = code_ref[k, META - TAIL + s]
            at = jnp.maximum(code, 0)
            where = jnp.where(code >= 0, k, TILES)
            rows = pl.ds(pl.multiple_of((at // BT) * ROWS, 16), ROWS)
            lanes = pl.ds(pl.multiple_of((at % BT) * LANES, LANES), BLK)
            out_ref[where, rows, lanes] = wire[:, s * BLK:(s + 1) * BLK]
        return carry

    lax.fori_loop(0, TILES, tile, 0)


def unpack_right(code_ref, which, wire_ref, right_ref, first_row):
    def tile(k, carry):
        wire = wire_ref[k, pl.ds(first_row, COLS), :]
        row = k // 4 * 4 + k % 2 * 2 + k // 2 % 2
        for s in range(CAP):
            code = code_ref[k, META - TAIL + which * CAP + s]
            at = jnp.maximum(code, 0)
            where = jnp.where(code >= 0, row, TILES)
            rows = pl.ds(pl.multiple_of((at % BT) * COLS, 16), COLS)
            lanes = pl.ds(pl.multiple_of((at // BT) * LANES, LANES), BLK)
            right_ref[where, rows, lanes] = wire[:, s * BLK:(s + 1) * BLK]
        return carry

    lax.fori_loop(0, TILES, tile, 0)


def parts(src_ref, dst_ref, sems):
    return [
        pltpu.make_async_copy(
            src_ref.at[pl.ds(n * BT, BT)], dst_ref.at[pl.ds(n * BT, BT)], sems.at[n]
        )
        for n in range(TILES // BT)
    ]


def multiply(ham_ref, right_ref, before=None):
    total = jnp.zeros((BT * ROWS, BT * COLS), F32)
    for n in range(TILES // BT):
        if before:
            before[n].wait()
        for k in range(n * BT, (n + 1) * BT):
            total = total + dot_nt(ham_ref[k], right_ref[k])
    return total


def product(ham_hbm, ham_ref, sems, code_ref, which, wire_ref, right_ref):
    copies = parts(ham_hbm, ham_ref, sems)
    for one in copies:
        one.start()
    right_ref[...] = jnp.zeros_like(right_ref)
    unpack_right(code_ref, which, wire_ref, right_ref, 0)
    return multiply(ham_ref, right_ref, copies)


def keep(codes, total):
    row = lax.broadcasted_iota(jnp.int32, total.shape, 0) // ROWS
    col = lax.broadcasted_iota(jnp.int32, total.shape, 1) // COLS
    place = row * BT + col
    kept = place == codes[0]
    for s in range(1, CAP):
        kept = kept | (place == codes[s])
    return jnp.where(kept, total, 0.0)


def pack(codes, term, rounded_ref, wire_ref):
    rounded_ref[...] = term.astype(BF)
    pieces = []
    for s in range(CAP):
        at = jnp.maximum(codes[s], 0)
        pick = one_hot((COLS, BT * COLS), (at % BT) * COLS, COLS)
        rows = pl.ds(pl.multiple_of((at // BT) * ROWS, 16), ROWS)
        pieces.append(dot_nt(pick, rounded_ref[rows, :]).astype(BF)[:, 0:BLK])
    pieces.append(jnp.zeros((COLS, WIRE - META), BF))
    wire_ref[...] = jnp.concatenate(pieces, axis=1)


def all_codes(index_ref, count_ref):
    return [code_of(index_ref, count_ref, s) for s in range(CAP)]


def first_kernel(index_ref, count_ref, own_ref, other_ref, ham_out, code_out, term_ref, out_ref,
                 ham_ref, right_ref, rounded_ref, note_ref, hcode_ref, dcode_ref, sems):
    layer = lax.axis_index("layer")
    for k in range(TILES):
        own = own_ref[k, 0:16, TAIL:][0:1].astype(F32).astype(jnp.int32)
        other = other_ref[k, 0:16, TAIL:][0:1].astype(F32).astype(jnp.int32)
        note_ref[0, k:k + 1, :] = jnp.where(layer == 0, own, other)
        note_ref[1, k:k + 1, :] = jnp.where(layer == 0, other, own)
    code_out[...] = note_ref[0]
    dens_codes = pltpu.make_async_copy(note_ref.at[0], dcode_ref, sems.at[0])
    ham_codes = pltpu.make_async_copy(note_ref.at[1], hcode_ref, sems.at[1])
    dens_codes.start()
    ham_codes.start()
    ham_ref[...] = jnp.zeros_like(ham_ref)
    right_ref[...] = jnp.zeros_like(right_ref)
    dens_codes.wait()
    ham_codes.wait()
    pl.when(layer == 1)(lambda: unpack_ham(hcode_ref, own_ref, ham_ref))
    pl.when(layer == 0)(lambda: unpack_ham(hcode_ref, other_ref, ham_ref))
    copies = parts(ham_ref, ham_out, sems)
    for one in copies:
        one.start()
    pl.when(layer == 0)(lambda: unpack_right(dcode_ref, 0, own_ref, right_ref, 0))
    pl.when(layer == 1)(lambda: unpack_right(dcode_ref, 0, other_ref, right_ref, COLS))
    codes = all_codes(index_ref, count_ref)
    term = keep(codes, multiply(ham_ref, right_ref))
    term_ref[...] = term
    pack(codes, term, rounded_ref, out_ref)
    for one in copies:
        one.wait()


def second_kernel(code_ref, index_ref, count_ref, ham_hbm, wire_ref, dense_ref, real_ref, out_ref,
                  ham_ref, right_ref, rounded_ref, sems):
    codes = all_codes(index_ref, count_ref)
    term = keep(codes, product(ham_hbm, ham_ref, sems, code_ref, 1, wire_ref, right_ref))
    real_ref[...] = dense_ref[...] - 0.5 * term
    pack(codes, term, rounded_ref, out_ref)


def third_kernel(code_ref, index_ref, count_ref, ham_hbm, wire_ref, first_ref, imag_ref, ham_ref,
                 right_ref, sems):
    codes = all_codes(index_ref, count_ref)
    term = keep(codes, product(ham_hbm, ham_ref, sems, code_ref, 2, wire_ref, right_ref))
    imag_ref[...] = term / 6.0 - first_ref[...]


def join_kernel(own_ref, other_ref, out_ref):
    swap = lax.axis_index("layer") == 1
    own, other = own_ref[...], other_ref[...]
    low, high = jnp.where(swap, other, own), jnp.where(swap, own, other)
    pieces = []
    for j in range(BT):
        pieces += [low[:, j * COLS:j * COLS + HALF], high[:, j * COLS:j * COLS + HALF]]
    whole = jnp.concatenate(pieces, axis=1)
    for i in range(BT):
        out_ref[i * BLK:(i + 1) * BLK, :] = whole[i * ROWS:i * ROWS + BLK, :]


def call(kernel, in_specs, arrays, out_shape, scratch=(), out_specs=None, vmem=24 << 20):
    return pl.pallas_call(
        kernel,
        out_shape=out_shape,
        in_specs=in_specs,
        out_specs=out_specs or jax.tree.map(lambda _: VMEM, out_shape),
        scratch_shapes=list(scratch),
        compiler_params=pltpu.CompilerParams(vmem_limit_bytes=vmem),
    )(*arrays)


def shape(*dims, dtype=BF):
    return jax.ShapeDtypeStruct(dims, dtype)


def place(x, y_lo, z, y_hi, layer):
    return (((x * 4 + y_lo) * 8 + z) * 2 + y_hi) * 2 + layer


def everywhere():
    return list(itertools.product(range(4), range(4), range(8), range(2), range(2)))


def pair_route(both):
    route = []
    for x, y_lo, z, y_hi, layer in everywhere():
        to = (x, y_lo, z, 1 - y_hi, layer) if both and layer else (x, y_lo ^ 2, z, y_hi, layer)
        route.append((place(x, y_lo, z, y_hi, layer), place(*to)))
    return route


def groups(both):
    found = {}
    for x, y_lo, z, y_hi, layer in everywhere():
        key = (layer, x, y_lo, y_hi) if both and layer else (layer, y_lo // 2, z, y_hi)
        found.setdefault(key, []).append(place(x, y_lo, z, y_hi, layer))
    return sorted(found.values())


def gather(piece, first, both):
    far = lax.ppermute(piece, AXES, pair_route(both))
    pair = jnp.where(first, jnp.stack([piece, far]), jnp.stack([far, piece]))
    return lax.all_to_all(
        jnp.broadcast_to(pair, (8,) + pair.shape), AXES, 0, 0, axis_index_groups=groups(both)
    )


def swap(values):
    return lax.ppermute(values, "layer", [(0, 1), (1, 0)])


def per_device(ham_blocks, ham_index, ham_count, dens_blocks, dens_index, dens_count, first_index,
               first_count, second_index, second_count, third_index, third_count):
    layer = lax.axis_index("layer")
    y_first = lax.axis_index("y_lo") < 2
    index = pltpu.SMEM((2, 1, CAP), jnp.int32)
    packed = pltpu.VMEM((BLK, META), BF)
    payload = call(
        prep_kernel,
        [HBM, SMEM] * 4 + [HBM, HBM],
        (ham_index, ham_count, dens_index, dens_count, first_index, first_count, second_index,
         second_count, ham_blocks, dens_blocks),
        shape(ROWS, WIRE),
        [index] * 4 + [packed, packed, pltpu.SemaphoreType.DMA((6,))],
        vmem=62900000,
    )
    first = jnp.where(layer == 0, y_first, lax.axis_index("y_hi") == 0)
    panel = gather(payload, first, True)
    panel = panel.reshape((TILES,) + panel.shape[2:])
    other = swap(panel)
    half = shape(BT * ROWS, BT * COLS, dtype=F32)
    dense_half = call(
        dense_kernel, [SMEM, SMEM, VMEM], (dens_index, dens_count, dens_blocks), half
    )
    ham_shape = (TILES + 1, BT * ROWS, BT * LANES)
    dense_ham = pltpu.VMEM(ham_shape, BF)
    dense_right = pltpu.VMEM((TILES + 1, BT * COLS, BT * LANES), BF)
    rounded = pltpu.VMEM((BT * ROWS, BT * COLS), BF)
    sems = pltpu.SemaphoreType.DMA((TILES // BT,))
    code = pltpu.SMEM((TILES, LANES), jnp.int32)
    wire = shape(COLS, WIRE)

    def gathered(piece):
        tiles = gather(piece, y_first, False)
        return tiles.reshape((TILES,) + tiles.shape[2:])

    ham, codes, first_term, first_wire = call(
        first_kernel,
        [SMEM, SMEM, VMEM, VMEM],
        (first_index, first_count, panel, other),
        (shape(*ham_shape), shape(TILES, LANES, dtype=jnp.int32), half, wire),
        [dense_ham, dense_right, rounded, pltpu.VMEM((2, TILES, LANES), jnp.int32), code, code, sems],
        (HBM, VMEM, VMEM, VMEM),
    )
    real_half, second_wire = call(
        second_kernel,
        [SMEM, SMEM, SMEM, HBM, VMEM, VMEM],
        (codes, second_index, second_count, ham, gathered(first_wire), dense_half),
        (half, wire),
        [dense_ham, dense_right, rounded, sems],
    )
    real_part = join(real_half)
    imag_half = call(
        third_kernel,
        [SMEM, SMEM, SMEM, HBM, VMEM, VMEM],
        (codes, third_index, third_count, ham, gathered(second_wire), first_term),
        half,
        [dense_ham, dense_right, sems],
    )
    return real_part, join(imag_half)


def join(part):
    return call(join_kernel, [VMEM, VMEM], (part, swap(part)), shape(SIDE, SIDE, dtype=F32))


def solution(mesh):
    split = Mesh(mesh.devices.reshape(4, 4, 8, 2, 2), AXES)
    row, col = ("x", "y_lo"), ("z", "y_hi")
    blocks, index = P(row, col), P(None, row, col)
    in_specs = (blocks, index, blocks) * 2 + (index, blocks) * 3
    return jax.shard_map(
        per_device, mesh=split, in_specs=in_specs, out_specs=(blocks, blocks), check_vma=False
    )
```

```python
import itertools

import jax
import jax.numpy as jnp
from jax import lax
from jax.experimental import pallas as pl
from jax.experimental.pallas import tpu as pltpu
from jax.sharding import Mesh, PartitionSpec as P

BLK = 92
HALF = 46
BT = 4
CAP = 8
ROWS = 96
COLS = 48
LANES = 128
SIDE = BT * BLK
WIRE = 768
META = 736
TAIL = WIRE - LANES
TILES = 16
AXES = ("x", "y_lo", "z", "y_hi", "layer")
BF = jnp.bfloat16
F32 = jnp.float32
VMEM = pl.BlockSpec(memory_space=pltpu.VMEM)
SMEM = pl.BlockSpec(memory_space=pltpu.SMEM)
HBM = pl.BlockSpec(memory_space=pltpu.HBM)


def dot_nt(a, b):
    return lax.dot_general(a, b, (((1,), (1,)), ((), ())), preferred_element_type=F32)


def one_hot(shape, shift, width):
    q = lax.broadcasted_iota(jnp.int32, shape, 0)
    x = lax.broadcasted_iota(jnp.int32, shape, 1)
    return jnp.where((x == q + shift) & (q < width), 1.0, 0.0).astype(BF)


def code_of(index_ref, count_ref, s):
    return jnp.where(s < count_ref[0, 0], index_ref[0, 0, s] * BT + index_ref[1, 0, s], -1)


def prep_kernel(hidx_hbm, hcnt_ref, didx_hbm, dcnt_ref, fidx_hbm, fcnt_ref, sidx_hbm, scnt_ref,
                ham_hbm, dens_hbm, out_ref, hidx_ref, didx_ref, fidx_ref, sidx_ref, ham_ref,
                dens_ref, sems):
    pairs = ((ham_hbm, ham_ref), (dens_hbm, dens_ref), (hidx_hbm, hidx_ref), (didx_hbm, didx_ref),
             (fidx_hbm, fidx_ref), (sidx_hbm, sidx_ref))
    copies = [pltpu.make_async_copy(src, dst, sems.at[n]) for n, (src, dst) in enumerate(pairs)]
    for one in copies:
        one.start()
    for one in copies:
        one.wait()
    layer = lax.axis_index("layer")
    lane = lax.broadcasted_iota(jnp.int32, (ROWS, LANES), 1) - (META - TAIL)

    def noted(tail, *lists):
        for n, (index_ref, count_ref) in enumerate(lists):
            for s in range(CAP):
                code = code_of(index_ref, count_ref, s).astype(F32)
                tail = jnp.where(lane == n * CAP + s, code, tail)
        return tail.astype(BF)

    @pl.when(layer == 0)
    def _():
        dens = dens_ref[...]
        r = lax.broadcasted_iota(jnp.int32, (2 * COLS, META), 0)
        x = lax.broadcasted_iota(jnp.int32, (2 * COLS, META), 1)
        q = r % COLS
        pieces = []
        for s in range(CAP):
            pick = (x == q + (r // COLS) * HALF + s * BLK) & (q < HALF)
            pieces.append(dot_nt(jnp.where(pick, 1.0, 0.0).astype(BF), dens))
        pieces.append(jnp.zeros((2 * COLS, WIRE - META), F32))
        wire = jnp.concatenate(pieces, axis=1)
        out_ref[:, 0:TAIL] = wire[:, 0:TAIL].astype(BF)
        out_ref[:, TAIL:] = noted(
            wire[:, TAIL:], (didx_ref, dcnt_ref), (fidx_ref, fcnt_ref), (sidx_ref, scnt_ref)
        )

    @pl.when(layer == 1)
    def _():
        out_ref[...] = jnp.zeros_like(out_ref)
        out_ref[0:BLK, 0:META] = ham_ref[...]
        tail = out_ref[:, TAIL:].astype(F32)
        out_ref[:, TAIL:] = noted(tail, (hidx_ref, hcnt_ref))


def dense_kernel(didx_ref, dcnt_ref, dens_ref, dense_ref):
    layer = lax.axis_index("layer")
    dens = dens_ref[...]
    dense_ref[...] = jnp.zeros_like(dense_ref)
    for s in range(CAP):
        code = code_of(didx_ref, dcnt_ref, s)
        at = jnp.maximum(code, 0)
        i, j = at // BT, at % BT
        x = lax.broadcasted_iota(jnp.int32, (META, BT * COLS), 0)
        y = lax.broadcasted_iota(jnp.int32, (META, BT * COLS), 1) - j * COLS
        spread = jnp.where(
            (x == y + (s * BLK + layer * HALF)) & (y >= 0) & (y < HALF) & (code >= 0), 1.0, 0.0
        ).astype(BF)
        block = jnp.dot(dens, spread, preferred_element_type=F32)
        block = jnp.concatenate([block, jnp.zeros((ROWS - BLK, BT * COLS), F32)], axis=0)
        rows = pl.ds(pl.multiple_of(i * ROWS, ROWS), ROWS)
        dense_ref[rows, :] = dense_ref[rows, :] + block


def unpack_ham(code_ref, from_ref, out_ref):
    def tile(k, carry):
        wire = from_ref[k]
        for s in range(CAP):
            code = code_ref[k, META - TAIL + s]
            at = jnp.maximum(code, 0)
            where = jnp.where(code >= 0, k, TILES)
            rows = pl.ds(pl.multiple_of((at // BT) * ROWS, 16), ROWS)
            lanes = pl.ds(pl.multiple_of((at % BT) * LANES, LANES), BLK)
            out_ref[where, rows, lanes] = wire[:, s * BLK:(s + 1) * BLK]
        return carry

    lax.fori_loop(0, TILES, tile, 0)


def unpack_right(code_ref, which, wire_ref, right_ref, first_row):
    def tile(k, carry):
        wire = wire_ref[k, pl.ds(first_row, COLS), :]
        row = k // 4 * 4 + k % 2 * 2 + k // 2 % 2
        for s in range(CAP):
            code = code_ref[k, META - TAIL + which * CAP + s]
            at = jnp.maximum(code, 0)
            where = jnp.where(code >= 0, row, TILES)
            rows = pl.ds(pl.multiple_of((at % BT) * COLS, 16), COLS)
            lanes = pl.ds(pl.multiple_of((at // BT) * LANES, LANES), BLK)
            right_ref[where, rows, lanes] = wire[:, s * BLK:(s + 1) * BLK]
        return carry

    lax.fori_loop(0, TILES, tile, 0)


def parts(src_ref, dst_ref, sems):
    return [
        pltpu.make_async_copy(
            src_ref.at[pl.ds(n * BT, BT)], dst_ref.at[pl.ds(n * BT, BT)], sems.at[n]
        )
        for n in range(TILES // BT)
    ]


def multiply(ham_ref, right_ref, before=None):
    total = jnp.zeros((BT * ROWS, BT * COLS), F32)
    for n in range(TILES // BT):
        if before:
            before[n].wait()
        for k in range(n * BT, (n + 1) * BT):
            total = total + dot_nt(ham_ref[k], right_ref[k])
    return total


def product(ham_hbm, ham_ref, sems, code_ref, which, wire_ref, right_ref):
    copies = parts(ham_hbm, ham_ref, sems)
    for one in copies:
        one.start()
    right_ref[...] = jnp.zeros_like(right_ref)
    unpack_right(code_ref, which, wire_ref, right_ref, 0)
    return multiply(ham_ref, right_ref, copies)


def keep(codes, total):
    row = lax.broadcasted_iota(jnp.int32, total.shape, 0) // ROWS
    col = lax.broadcasted_iota(jnp.int32, total.shape, 1) // COLS
    place = row * BT + col
    kept = place == codes[0]
    for s in range(1, CAP):
        kept = kept | (place == codes[s])
    return jnp.where(kept, total, 0.0)


def pack(codes, term, rounded_ref, wire_ref):
    rounded_ref[...] = term.astype(BF)
    pieces = []
    for s in range(CAP):
        at = jnp.maximum(codes[s], 0)
        pick = one_hot((COLS, BT * COLS), (at % BT) * COLS, COLS)
        rows = pl.ds(pl.multiple_of((at // BT) * ROWS, 16), ROWS)
        pieces.append(dot_nt(pick, rounded_ref[rows, :]).astype(BF)[:, 0:BLK])
    pieces.append(jnp.zeros((COLS, WIRE - META), BF))
    wire_ref[...] = jnp.concatenate(pieces, axis=1)


def all_codes(index_ref, count_ref):
    return [code_of(index_ref, count_ref, s) for s in range(CAP)]


def first_kernel(index_ref, count_ref, own_ref, other_ref, ham_out, code_out, term_ref, out_ref,
                 ham_ref, right_ref, rounded_ref, note_ref, hcode_ref, dcode_ref, sems):
    layer = lax.axis_index("layer")
    for k in range(TILES):
        own = own_ref[k, 0:16, TAIL:][0:1].astype(F32).astype(jnp.int32)
        other = other_ref[k, 0:16, TAIL:][0:1].astype(F32).astype(jnp.int32)
        note_ref[0, k:k + 1, :] = jnp.where(layer == 0, own, other)
        note_ref[1, k:k + 1, :] = jnp.where(layer == 0, other, own)
    code_out[...] = note_ref[0]
    dens_codes = pltpu.make_async_copy(note_ref.at[0], dcode_ref, sems.at[0])
    ham_codes = pltpu.make_async_copy(note_ref.at[1], hcode_ref, sems.at[1])
    dens_codes.start()
    ham_codes.start()
    ham_ref[...] = jnp.zeros_like(ham_ref)
    right_ref[...] = jnp.zeros_like(right_ref)
    dens_codes.wait()
    ham_codes.wait()
    pl.when(layer == 1)(lambda: unpack_ham(hcode_ref, own_ref, ham_ref))
    pl.when(layer == 0)(lambda: unpack_ham(hcode_ref, other_ref, ham_ref))
    copies = parts(ham_ref, ham_out, sems)
    for one in copies:
        one.start()
    pl.when(layer == 0)(lambda: unpack_right(dcode_ref, 0, own_ref, right_ref, 0))
    pl.when(layer == 1)(lambda: unpack_right(dcode_ref, 0, other_ref, right_ref, COLS))
    codes = all_codes(index_ref, count_ref)
    term = keep(codes, multiply(ham_ref, right_ref))
    term_ref[...] = term
    pack(codes, term, rounded_ref, out_ref)
    for one in copies:
        one.wait()


def second_kernel(code_ref, index_ref, count_ref, ham_hbm, wire_ref, dense_ref, real_ref, out_ref,
                  ham_ref, right_ref, rounded_ref, sems):
    codes = all_codes(index_ref, count_ref)
    term = keep(codes, product(ham_hbm, ham_ref, sems, code_ref, 1, wire_ref, right_ref))
    real_ref[...] = dense_ref[...] - 0.5 * term
    pack(codes, term, rounded_ref, out_ref)


def third_kernel(code_ref, index_ref, count_ref, ham_hbm, wire_ref, first_ref, joined_ref, imag_ref,
                 ham_ref, right_ref, sems):
    del joined_ref
    codes = all_codes(index_ref, count_ref)
    term = keep(codes, product(ham_hbm, ham_ref, sems, code_ref, 2, wire_ref, right_ref))
    imag_ref[...] = term / 6.0 - first_ref[...]


def join_kernel(own_ref, other_ref, out_ref, done_ref):
    done_ref[...] = jnp.zeros_like(done_ref)
    swap = lax.axis_index("layer") == 1
    own, other = own_ref[...], other_ref[...]
    low, high = jnp.where(swap, other, own), jnp.where(swap, own, other)
    pieces = []
    for j in range(BT):
        pieces += [low[:, j * COLS:j * COLS + HALF], high[:, j * COLS:j * COLS + HALF]]
    whole = jnp.concatenate(pieces, axis=1)
    for i in range(BT):
        out_ref[i * BLK:(i + 1) * BLK, :] = whole[i * ROWS:i * ROWS + BLK, :]


def call(kernel, in_specs, arrays, out_shape, scratch=(), out_specs=None, vmem=24 << 20):
    return pl.pallas_call(
        kernel,
        out_shape=out_shape,
        in_specs=in_specs,
        out_specs=out_specs or jax.tree.map(lambda _: VMEM, out_shape),
        scratch_shapes=list(scratch),
        compiler_params=pltpu.CompilerParams(vmem_limit_bytes=vmem),
    )(*arrays)


def shape(*dims, dtype=BF):
    return jax.ShapeDtypeStruct(dims, dtype)


def place(x, y_lo, z, y_hi, layer):
    return (((x * 4 + y_lo) * 8 + z) * 2 + y_hi) * 2 + layer


def everywhere():
    return list(itertools.product(range(4), range(4), range(8), range(2), range(2)))


def pair_route(both):
    route = []
    for x, y_lo, z, y_hi, layer in everywhere():
        to = (x, y_lo, z, 1 - y_hi, layer) if both and layer else (x, y_lo ^ 2, z, y_hi, layer)
        route.append((place(x, y_lo, z, y_hi, layer), place(*to)))
    return route


def groups(both):
    found = {}
    for x, y_lo, z, y_hi, layer in everywhere():
        key = (layer, x, y_lo, y_hi) if both and layer else (layer, y_lo // 2, z, y_hi)
        found.setdefault(key, []).append(place(x, y_lo, z, y_hi, layer))
    return sorted(found.values())


def gather(piece, first, both):
    far = lax.ppermute(piece, AXES, pair_route(both))
    pair = jnp.where(first, jnp.stack([piece, far]), jnp.stack([far, piece]))
    return lax.all_to_all(
        jnp.broadcast_to(pair, (8,) + pair.shape), AXES, 0, 0, axis_index_groups=groups(both)
    )


def swap(values):
    return lax.ppermute(values, "layer", [(0, 1), (1, 0)])


def per_device(ham_blocks, ham_index, ham_count, dens_blocks, dens_index, dens_count, first_index,
               first_count, second_index, second_count, third_index, third_count):
    layer = lax.axis_index("layer")
    y_first = lax.axis_index("y_lo") < 2
    index = pltpu.SMEM((2, 1, CAP), jnp.int32)
    packed = pltpu.VMEM((BLK, META), BF)
    payload = call(
        prep_kernel,
        [HBM, SMEM] * 4 + [HBM, HBM],
        (ham_index, ham_count, dens_index, dens_count, first_index, first_count, second_index,
         second_count, ham_blocks, dens_blocks),
        shape(ROWS, WIRE),
        [index] * 4 + [packed, packed, pltpu.SemaphoreType.DMA((6,))],
        vmem=62900000,
    )
    first = jnp.where(layer == 0, y_first, lax.axis_index("y_hi") == 0)
    panel = gather(payload, first, True)
    panel = panel.reshape((TILES,) + panel.shape[2:])
    other = swap(panel)
    half = shape(BT * ROWS, BT * COLS, dtype=F32)
    dense_half = call(
        dense_kernel, [SMEM, SMEM, VMEM], (dens_index, dens_count, dens_blocks), half
    )
    ham_shape = (TILES + 1, BT * ROWS, BT * LANES)
    dense_ham = pltpu.VMEM(ham_shape, BF)
    dense_right = pltpu.VMEM((TILES + 1, BT * COLS, BT * LANES), BF)
    rounded = pltpu.VMEM((BT * ROWS, BT * COLS), BF)
    sems = pltpu.SemaphoreType.DMA((TILES // BT,))
    code = pltpu.SMEM((TILES, LANES), jnp.int32)
    wire = shape(COLS, WIRE)

    def gathered(piece):
        tiles = gather(piece, y_first, False)
        return tiles.reshape((TILES,) + tiles.shape[2:])

    ham, codes, first_term, first_wire = call(
        first_kernel,
        [SMEM, SMEM, VMEM, VMEM],
        (first_index, first_count, panel, other),
        (shape(*ham_shape), shape(TILES, LANES, dtype=jnp.int32), half, wire),
        [dense_ham, dense_right, rounded, pltpu.VMEM((2, TILES, LANES), jnp.int32), code, code, sems],
        (HBM, VMEM, VMEM, VMEM),
        vmem=45 << 20,
    )
    real_half, second_wire = call(
        second_kernel,
        [SMEM, SMEM, SMEM, HBM, VMEM, VMEM],
        (codes, second_index, second_count, ham, gathered(first_wire), dense_half),
        (half, wire),
        [dense_ham, dense_right, rounded, sems],
        vmem=50 << 20,
    )
    real_part, joined = join(real_half)
    imag_half = call(
        third_kernel,
        [SMEM, SMEM, SMEM, HBM, VMEM, VMEM, VMEM],
        (codes, third_index, third_count, ham, gathered(second_wire), first_term, joined),
        half,
        [dense_ham, dense_right, sems],
        vmem=50 << 20,
    )
    return real_part, join(imag_half)[0]


def join(part):
    return call(
        join_kernel, [VMEM, VMEM], (part, swap(part)),
        (shape(SIDE, SIDE, dtype=F32), shape(8, LANES, dtype=F32)),
    )


def solution(mesh):
    split = Mesh(mesh.devices.reshape(4, 4, 8, 2, 2), AXES)
    row, col = ("x", "y_lo"), ("z", "y_hi")
    blocks, index = P(row, col), P(None, row, col)
    in_specs = (blocks, index, blocks) * 2 + (index, blocks) * 3
    return jax.shard_map(
        per_device, mesh=split, in_specs=in_specs, out_specs=(blocks, blocks), check_vma=False
    )
```

```python
import itertools

import jax
import jax.numpy as jnp
from jax import lax
from jax.experimental import pallas as pl
from jax.experimental.pallas import tpu as pltpu
from jax.sharding import Mesh, PartitionSpec as P

BLK = 92
HALF = 46
BT = 4
CAP = 8
ROWS = 96
COLS = 48
LANES = 128
SIDE = BT * BLK
WIRE = 768
META = 736
TAIL = WIRE - LANES
TILES = 16
AXES = ("x", "y_lo", "z", "y_hi", "layer")
BF = jnp.bfloat16
F32 = jnp.float32
VMEM = pl.BlockSpec(memory_space=pltpu.VMEM)
SMEM = pl.BlockSpec(memory_space=pltpu.SMEM)
HBM = pl.BlockSpec(memory_space=pltpu.HBM)


def dot_nt(a, b):
    return lax.dot_general(a, b, (((1,), (1,)), ((), ())), preferred_element_type=F32)


def one_hot(shape, shift, width):
    q = lax.broadcasted_iota(jnp.int32, shape, 0)
    x = lax.broadcasted_iota(jnp.int32, shape, 1)
    return jnp.where((x == q + shift) & (q < width), 1.0, 0.0).astype(BF)


def code_of(index_ref, count_ref, s):
    return jnp.where(s < count_ref[0, 0], index_ref[0, 0, s] * BT + index_ref[1, 0, s], -1)


def prep_kernel(hidx_hbm, hcnt_ref, didx_hbm, dcnt_ref, fidx_hbm, fcnt_ref, sidx_hbm, scnt_ref,
                ham_hbm, dens_hbm, out_ref, hidx_ref, didx_ref, fidx_ref, sidx_ref, ham_ref,
                dens_ref, sems):
    pairs = ((ham_hbm, ham_ref), (dens_hbm, dens_ref), (hidx_hbm, hidx_ref), (didx_hbm, didx_ref),
             (fidx_hbm, fidx_ref), (sidx_hbm, sidx_ref))
    copies = [pltpu.make_async_copy(src, dst, sems.at[n]) for n, (src, dst) in enumerate(pairs)]
    for one in copies:
        one.start()
    for one in copies:
        one.wait()
    layer = lax.axis_index("layer")
    lane = lax.broadcasted_iota(jnp.int32, (ROWS, LANES), 1) - (META - TAIL)

    def noted(tail, *lists):
        for n, (index_ref, count_ref) in enumerate(lists):
            for s in range(CAP):
                code = code_of(index_ref, count_ref, s).astype(F32)
                tail = jnp.where(lane == n * CAP + s, code, tail)
        return tail.astype(BF)

    @pl.when(layer == 0)
    def _():
        dens = dens_ref[...]
        r = lax.broadcasted_iota(jnp.int32, (2 * COLS, META), 0)
        x = lax.broadcasted_iota(jnp.int32, (2 * COLS, META), 1)
        q = r % COLS
        pieces = []
        for s in range(CAP):
            pick = (x == q + (r // COLS) * HALF + s * BLK) & (q < HALF)
            pieces.append(dot_nt(jnp.where(pick, 1.0, 0.0).astype(BF), dens))
        pieces.append(jnp.zeros((2 * COLS, WIRE - META), F32))
        wire = jnp.concatenate(pieces, axis=1)
        out_ref[:, 0:TAIL] = wire[:, 0:TAIL].astype(BF)
        out_ref[:, TAIL:] = noted(
            wire[:, TAIL:], (didx_ref, dcnt_ref), (fidx_ref, fcnt_ref), (sidx_ref, scnt_ref)
        )

    @pl.when(layer == 1)
    def _():
        out_ref[...] = jnp.zeros_like(out_ref)
        out_ref[0:BLK, 0:META] = ham_ref[...]
        tail = out_ref[:, TAIL:].astype(F32)
        out_ref[:, TAIL:] = noted(tail, (hidx_ref, hcnt_ref))


def dense_kernel(didx_ref, dcnt_ref, dens_ref, dense_ref):
    layer = lax.axis_index("layer")
    dens = dens_ref[...]
    dense_ref[...] = jnp.zeros_like(dense_ref)
    for s in range(CAP):
        code = code_of(didx_ref, dcnt_ref, s)
        at = jnp.maximum(code, 0)
        i, j = at // BT, at % BT
        x = lax.broadcasted_iota(jnp.int32, (META, BT * COLS), 0)
        y = lax.broadcasted_iota(jnp.int32, (META, BT * COLS), 1) - j * COLS
        spread = jnp.where(
            (x == y + (s * BLK + layer * HALF)) & (y >= 0) & (y < HALF) & (code >= 0), 1.0, 0.0
        ).astype(BF)
        block = jnp.dot(dens, spread, preferred_element_type=F32)
        block = jnp.concatenate([block, jnp.zeros((ROWS - BLK, BT * COLS), F32)], axis=0)
        rows = pl.ds(pl.multiple_of(i * ROWS, ROWS), ROWS)
        dense_ref[rows, :] = dense_ref[rows, :] + block


def unpack_ham(code_ref, g, from_ref, ham_ref):
    ham_ref[...] = jnp.zeros_like(ham_ref)
    for t in range(BT):
        wire = from_ref[g * BT + t]
        for s in range(CAP):
            code = code_ref[g * BT + t, META - TAIL + s]
            at = jnp.maximum(code, 0)
            where = jnp.where(code >= 0, t, BT)
            rows = pl.ds(pl.multiple_of((at // BT) * ROWS, 16), ROWS)
            lanes = pl.ds(pl.multiple_of((at % BT) * LANES, LANES), BLK)
            ham_ref[where, rows, lanes] = wire[:, s * BLK:(s + 1) * BLK]


def unpack_right(code_ref, which, g, wire_ref, right_ref, first_row=0):
    right_ref[...] = jnp.zeros_like(right_ref)
    for t in range(BT):
        wire = wire_ref[g * BT + t, pl.ds(first_row, COLS), :]
        for s in range(CAP):
            code = code_ref[g * BT + t, META - TAIL + which * CAP + s]
            at = jnp.maximum(code, 0)
            where = jnp.where(code >= 0, t % 2 * 2 + t // 2, BT)
            rows = pl.ds(pl.multiple_of((at % BT) * COLS, 16), COLS)
            lanes = pl.ds(pl.multiple_of((at // BT) * LANES, LANES), BLK)
            right_ref[where, rows, lanes] = wire[:, s * BLK:(s + 1) * BLK]


def multiply(total, ham_ref, right_ref):
    for t in range(BT):
        total = total + dot_nt(ham_ref[t], right_ref[t])
    return total


def product(ham_refs, code_ref, which, wire_ref, right_refs):
    total = jnp.zeros((BT * ROWS, BT * COLS), F32)
    unpack_right(code_ref, which, 0, wire_ref, right_refs[0])
    for g in range(BT):
        total = multiply(total, ham_refs[g], right_refs[g])
        if g + 1 < BT:
            unpack_right(code_ref, which, g + 1, wire_ref, right_refs[g + 1])
    return total


def keep(codes, total):
    row = lax.broadcasted_iota(jnp.int32, total.shape, 0) // ROWS
    col = lax.broadcasted_iota(jnp.int32, total.shape, 1) // COLS
    place = row * BT + col
    kept = place == codes[0]
    for s in range(1, CAP):
        kept = kept | (place == codes[s])
    return jnp.where(kept, total, 0.0)


def pack(codes, term, rounded_ref, wire_ref):
    rounded_ref[...] = term.astype(BF)
    pieces = []
    for s in range(CAP):
        at = jnp.maximum(codes[s], 0)
        pick = one_hot((COLS, BT * COLS), (at % BT) * COLS, COLS)
        rows = pl.ds(pl.multiple_of((at // BT) * ROWS, 16), ROWS)
        pieces.append(dot_nt(pick, rounded_ref[rows, :]).astype(BF)[:, 0:BLK])
    pieces.append(jnp.zeros((COLS, WIRE - META), BF))
    wire_ref[...] = jnp.concatenate(pieces, axis=1)


def all_codes(index_ref, count_ref):
    return [code_of(index_ref, count_ref, s) for s in range(CAP)]


def first_kernel(index_ref, count_ref, own_ref, other_ref, dense_ref, *refs):
    del dense_ref
    ham_refs, (code_out, term_ref, out_ref), right_refs = refs[0:4], refs[4:7], refs[7:11]
    rounded_ref, note_ref, hcode_ref, dcode_ref, sems = refs[11:]
    layer = lax.axis_index("layer")
    for k in range(TILES):
        own = own_ref[k, 0:16, TAIL:][0:1].astype(F32).astype(jnp.int32)
        other = other_ref[k, 0:16, TAIL:][0:1].astype(F32).astype(jnp.int32)
        note_ref[0, k:k + 1, :] = jnp.where(layer == 0, own, other)
        note_ref[1, k:k + 1, :] = jnp.where(layer == 0, other, own)
    code_out[...] = note_ref[0]
    dens_codes = pltpu.make_async_copy(note_ref.at[0], dcode_ref, sems.at[0])
    ham_codes = pltpu.make_async_copy(note_ref.at[1], hcode_ref, sems.at[1])
    dens_codes.start()
    ham_codes.start()
    dens_codes.wait()
    ham_codes.wait()

    def unpack(ham_from, dens_from, first_row):
        for g in range(BT):
            unpack_right(dcode_ref, 0, g, dens_from, right_refs[g], first_row)
            unpack_ham(hcode_ref, g, ham_from, ham_refs[g])

    pl.when(layer == 0)(lambda: unpack(other_ref, own_ref, 0))
    pl.when(layer == 1)(lambda: unpack(own_ref, other_ref, COLS))
    total = jnp.zeros((BT * ROWS, BT * COLS), F32)
    for g in range(BT):
        total = multiply(total, ham_refs[g], right_refs[g])
    codes = all_codes(index_ref, count_ref)
    term = keep(codes, total)
    term_ref[...] = term
    pack(codes, term, rounded_ref, out_ref)


def second_kernel(code_ref, index_ref, count_ref, h0, h1, h2, h3, wire_ref, dense_ref, real_ref,
                  out_ref, r0, r1, r2, r3, rounded_ref):
    codes = all_codes(index_ref, count_ref)
    term = keep(codes, product((h0, h1, h2, h3), code_ref, 1, wire_ref, (r0, r1, r2, r3)))
    real_ref[...] = dense_ref[...] - 0.5 * term
    pack(codes, term, rounded_ref, out_ref)


def third_kernel(code_ref, index_ref, count_ref, h0, h1, h2, h3, wire_ref, first_ref, real_ref,
                 halves_ref, r0, r1, r2, r3):
    codes = all_codes(index_ref, count_ref)
    halves_ref[0] = real_ref[...]
    term = keep(codes, product((h0, h1, h2, h3), code_ref, 2, wire_ref, (r0, r1, r2, r3)))
    halves_ref[1] = term / 6.0 - first_ref[...]


def join_kernel(own_ref, other_ref, *out_refs):
    swap = lax.axis_index("layer") == 1
    for n, out_ref in enumerate(out_refs):
        own, other = own_ref[n], other_ref[n]
        low, high = jnp.where(swap, other, own), jnp.where(swap, own, other)
        pieces = []
        for j in range(BT):
            pieces += [low[:, j * COLS:j * COLS + HALF], high[:, j * COLS:j * COLS + HALF]]
        whole = jnp.concatenate(pieces, axis=1)
        for i in range(BT):
            out_ref[i * BLK:(i + 1) * BLK, :] = whole[i * ROWS:i * ROWS + BLK, :]


def own_place(by_layer):
    high = lax.axis_index("y_lo") // 2
    if by_layer:
        high = jnp.where(lax.axis_index("layer") == 0, high, lax.axis_index("y_hi"))
    return high


def own_kernel(piece_ref, out_ref):
    at, piece = own_place(True), piece_ref[...]
    for n in range(out_ref.shape[0]):
        out_ref[n, at] = piece


def far_kernel(far_ref, pairs_ref, out_ref):
    del pairs_ref
    at, far = 1 - own_place(True), far_ref[...]
    for n in range(out_ref.shape[0]):
        out_ref[n, at] = far


def lay_kernel(piece_ref, far_ref, *refs):
    out_ref = refs[-1]
    at, piece, far = own_place(False), piece_ref[...], far_ref[...]
    for n in range(out_ref.shape[0]):
        out_ref[n, at] = piece
        out_ref[n, 1 - at] = far


def call(kernel, in_specs, arrays, out_shape, scratch=(), alias=None, vmem=24 << 20):
    return pl.pallas_call(
        kernel,
        out_shape=out_shape,
        in_specs=in_specs,
        out_specs=jax.tree.map(lambda _: VMEM, out_shape),
        input_output_aliases=alias or {},
        scratch_shapes=list(scratch),
        compiler_params=pltpu.CompilerParams(vmem_limit_bytes=vmem),
    )(*arrays)


def shape(*dims, dtype=BF):
    return jax.ShapeDtypeStruct(dims, dtype)


def place(x, y_lo, z, y_hi, layer):
    return (((x * 4 + y_lo) * 8 + z) * 2 + y_hi) * 2 + layer


def everywhere():
    return list(itertools.product(range(4), range(4), range(8), range(2), range(2)))


def pair_route(both):
    route = []
    for x, y_lo, z, y_hi, layer in everywhere():
        to = (x, y_lo, z, 1 - y_hi, layer) if both and layer else (x, y_lo ^ 2, z, y_hi, layer)
        route.append((place(x, y_lo, z, y_hi, layer), place(*to)))
    return route


def groups(both):
    found = {}
    for x, y_lo, z, y_hi, layer in everywhere():
        key = (layer, x, y_lo, y_hi) if both and layer else (layer, y_lo // 2, z, y_hi)
        found.setdefault(key, []).append(place(x, y_lo, z, y_hi, layer))
    return sorted(found.values())


def to_pair(piece, both):
    return lax.ppermute(piece, AXES, pair_route(both))


def spread(pairs, both):
    tiles = lax.all_to_all(pairs, AXES, 0, 0, axis_index_groups=groups(both))
    return tiles.reshape((TILES,) + tiles.shape[2:])


def swap(values):
    return lax.ppermute(values, "layer", [(0, 1), (1, 0)])


def per_device(ham_blocks, ham_index, ham_count, dens_blocks, dens_index, dens_count, first_index,
               first_count, second_index, second_count, third_index, third_count):
    index = pltpu.SMEM((2, 1, CAP), jnp.int32)
    packed = pltpu.VMEM((BLK, META), BF)
    payload = call(
        prep_kernel,
        [HBM, SMEM] * 4 + [HBM, HBM],
        (ham_index, ham_count, dens_index, dens_count, first_index, first_count, second_index,
         second_count, ham_blocks, dens_blocks),
        shape(ROWS, WIRE),
        [index] * 4 + [packed, packed, pltpu.SemaphoreType.DMA((6,))],
        vmem=62900000,
    )
    pairs = call(own_kernel, [VMEM], (payload,), shape(8, 2, ROWS, WIRE))
    pairs = call(
        far_kernel, [VMEM] * 2, (to_pair(payload, True), pairs), shape(8, 2, ROWS, WIRE),
        alias={1: 0},
    )
    panel = spread(pairs, True)
    half = shape(BT * ROWS, BT * COLS, dtype=F32)
    dense_half = call(
        dense_kernel, [SMEM, SMEM, VMEM], (dens_index, dens_count, dens_blocks), half
    )
    dense_ham = shape(BT + 1, BT * ROWS, BT * LANES)
    dense_right = [pltpu.VMEM((BT + 1, BT * COLS, BT * LANES), BF)] * BT
    rounded = pltpu.VMEM((BT * ROWS, BT * COLS), BF)
    code = pltpu.SMEM((TILES, LANES), jnp.int32)
    wire, wires = shape(COLS, WIRE), shape(8, 2, COLS, WIRE)
    *ham, codes, first_term, first_wire = call(
        first_kernel,
        [SMEM] * 2 + [VMEM] * 3,
        (first_index, first_count, panel, swap(panel), dense_half),
        (dense_ham,) * BT + (shape(TILES, LANES, dtype=jnp.int32), half, wire),
        dense_right + [rounded, pltpu.VMEM((2, TILES, LANES), jnp.int32), code, code,
                       pltpu.SemaphoreType.DMA((2,))],
    )
    pairs = call(lay_kernel, [VMEM] * 2, (first_wire, to_pair(first_wire, False)), wires)
    real_half, second_wire = call(
        second_kernel,
        [SMEM] * 3 + [VMEM] * 6,
        (codes, second_index, second_count, *ham, spread(pairs, False), dense_half),
        (half, wire),
        dense_right + [rounded],
    )
    pairs = call(
        lay_kernel,
        [VMEM, VMEM, SMEM],
        (second_wire, to_pair(second_wire, False), third_count),
        wires,
    )
    halves = call(
        third_kernel,
        [SMEM] * 3 + [VMEM] * 7,
        (codes, third_index, third_count, *ham, spread(pairs, False), first_term, real_half),
        shape(2, BT * ROWS, BT * COLS, dtype=F32),
        dense_right,
    )
    whole = shape(SIDE, SIDE, dtype=F32)
    return call(join_kernel, [VMEM] * 2, (halves, swap(halves)), (whole, whole))


def solution(mesh):
    split = Mesh(mesh.devices.reshape(4, 4, 8, 2, 2), AXES)
    row, col = ("x", "y_lo"), ("z", "y_hi")
    blocks, index = P(row, col), P(None, row, col)
    in_specs = (blocks, index, blocks) * 2 + (index, blocks) * 3
    return jax.shard_map(
        per_device, mesh=split, in_specs=in_specs, out_specs=(blocks, blocks), check_vma=False
    )
```

```python
import itertools

import jax
import jax.numpy as jnp
from jax import lax
from jax.experimental import pallas as pl
from jax.experimental.pallas import tpu as pltpu
from jax.sharding import Mesh, PartitionSpec as P

BLK = 92
HALF = 46
BT = 4
CAP = 8
ROWS = 96
COLS = 48
LANES = 128
SIDE = BT * BLK
WIRE = 768
META = 736
TAIL = WIRE - LANES
TILES = 16
AXES = ("x", "y_lo", "z", "y_hi", "layer")
BF = jnp.bfloat16
F32 = jnp.float32
VMEM = pl.BlockSpec(memory_space=pltpu.VMEM)
SMEM = pl.BlockSpec(memory_space=pltpu.SMEM)
HBM = pl.BlockSpec(memory_space=pltpu.HBM)


def dot_nt(a, b):
    return lax.dot_general(a, b, (((1,), (1,)), ((), ())), preferred_element_type=F32)


def one_hot(shape, shift, width):
    q = lax.broadcasted_iota(jnp.int32, shape, 0)
    x = lax.broadcasted_iota(jnp.int32, shape, 1)
    return jnp.where((x == q + shift) & (q < width), 1.0, 0.0).astype(BF)


def code_of(index_ref, count_ref, s):
    return jnp.where(s < count_ref[0, 0], index_ref[0, 0, s] * BT + index_ref[1, 0, s], -1)


def prep_kernel(hidx_hbm, hcnt_ref, didx_hbm, dcnt_ref, fidx_hbm, fcnt_ref, sidx_hbm, scnt_ref,
                ham_hbm, dens_hbm, out_ref, hidx_ref, didx_ref, fidx_ref, sidx_ref, ham_ref,
                dens_ref, sems):
    pairs = ((ham_hbm, ham_ref), (dens_hbm, dens_ref), (hidx_hbm, hidx_ref), (didx_hbm, didx_ref),
             (fidx_hbm, fidx_ref), (sidx_hbm, sidx_ref))
    copies = [pltpu.make_async_copy(src, dst, sems.at[n]) for n, (src, dst) in enumerate(pairs)]
    for one in copies:
        one.start()
    for one in copies:
        one.wait()
    layer = lax.axis_index("layer")
    lane = lax.broadcasted_iota(jnp.int32, (ROWS, LANES), 1) - (META - TAIL)

    def noted(tail, *lists):
        for n, (index_ref, count_ref) in enumerate(lists):
            for s in range(CAP):
                code = code_of(index_ref, count_ref, s).astype(F32)
                tail = jnp.where(lane == n * CAP + s, code, tail)
        return tail.astype(BF)

    @pl.when(layer == 0)
    def _():
        dens = dens_ref[...]
        r = lax.broadcasted_iota(jnp.int32, (2 * COLS, META), 0)
        x = lax.broadcasted_iota(jnp.int32, (2 * COLS, META), 1)
        q = r % COLS
        pieces = []
        for s in range(CAP):
            pick = (x == q + (r // COLS) * HALF + s * BLK) & (q < HALF)
            pieces.append(dot_nt(jnp.where(pick, 1.0, 0.0).astype(BF), dens))
        pieces.append(jnp.zeros((2 * COLS, WIRE - META), F32))
        wire = jnp.concatenate(pieces, axis=1)
        out_ref[:, 0:TAIL] = wire[:, 0:TAIL].astype(BF)
        out_ref[:, TAIL:] = noted(
            wire[:, TAIL:], (didx_ref, dcnt_ref), (fidx_ref, fcnt_ref), (sidx_ref, scnt_ref)
        )

    @pl.when(layer == 1)
    def _():
        out_ref[...] = jnp.zeros_like(out_ref)
        out_ref[0:BLK, 0:META] = ham_ref[...]
        tail = out_ref[:, TAIL:].astype(F32)
        out_ref[:, TAIL:] = noted(tail, (hidx_ref, hcnt_ref))


def dense_kernel(didx_ref, dcnt_ref, dens_ref, after_ref, dense_ref):
    del after_ref
    layer = lax.axis_index("layer")
    dens = dens_ref[...]
    dense_ref[...] = jnp.zeros_like(dense_ref)
    for s in range(CAP):
        code = code_of(didx_ref, dcnt_ref, s)
        at = jnp.maximum(code, 0)
        i, j = at // BT, at % BT
        x = lax.broadcasted_iota(jnp.int32, (META, BT * COLS), 0)
        y = lax.broadcasted_iota(jnp.int32, (META, BT * COLS), 1) - j * COLS
        spread = jnp.where(
            (x == y + (s * BLK + layer * HALF)) & (y >= 0) & (y < HALF) & (code >= 0), 1.0, 0.0
        ).astype(BF)
        block = jnp.dot(dens, spread, preferred_element_type=F32)
        block = jnp.concatenate([block, jnp.zeros((ROWS - BLK, BT * COLS), F32)], axis=0)
        rows = pl.ds(pl.multiple_of(i * ROWS, ROWS), ROWS)
        dense_ref[rows, :] = dense_ref[rows, :] + block


def unpack_ham(code_ref, g, from_ref, ham_ref):
    ham_ref[...] = jnp.zeros_like(ham_ref)
    for t in range(BT):
        wire = from_ref[g * BT + t]
        for s in range(CAP):
            code = code_ref[g * BT + t, META - TAIL + s]
            at = jnp.maximum(code, 0)
            where = jnp.where(code >= 0, t, BT)
            rows = pl.ds(pl.multiple_of((at // BT) * ROWS, 16), ROWS)
            lanes = pl.ds(pl.multiple_of((at % BT) * LANES, LANES), BLK)
            ham_ref[where, rows, lanes] = wire[:, s * BLK:(s + 1) * BLK]


def unpack_right(code_ref, which, g, wire_ref, right_ref, first_row=0):
    right_ref[...] = jnp.zeros_like(right_ref)
    for t in range(BT):
        wire = wire_ref[g * BT + t, pl.ds(first_row, COLS), :]
        for s in range(CAP):
            code = code_ref[g * BT + t, META - TAIL + which * CAP + s]
            at = jnp.maximum(code, 0)
            where = jnp.where(code >= 0, t % 2 * 2 + t // 2, BT)
            rows = pl.ds(pl.multiple_of((at % BT) * COLS, 16), COLS)
            lanes = pl.ds(pl.multiple_of((at // BT) * LANES, LANES), BLK)
            right_ref[where, rows, lanes] = wire[:, s * BLK:(s + 1) * BLK]


def multiply(total, ham_ref, right_ref):
    for t in range(BT):
        total = total + dot_nt(ham_ref[t], right_ref[t])
    return total


def product(ham_refs, code_ref, which, wire_ref, right_refs):
    total = jnp.zeros((BT * ROWS, BT * COLS), F32)
    unpack_right(code_ref, which, 0, wire_ref, right_refs[0])
    for g in range(BT):
        total = multiply(total, ham_refs[g], right_refs[g])
        if g + 1 < BT:
            unpack_right(code_ref, which, g + 1, wire_ref, right_refs[g + 1])
    return total


def keep(codes, total):
    row = lax.broadcasted_iota(jnp.int32, total.shape, 0) // ROWS
    col = lax.broadcasted_iota(jnp.int32, total.shape, 1) // COLS
    place = row * BT + col
    kept = place == codes[0]
    for s in range(1, CAP):
        kept = kept | (place == codes[s])
    return jnp.where(kept, total, 0.0)


def pack(codes, term, rounded_ref, wire_ref):
    rounded_ref[...] = term.astype(BF)
    pieces = []
    for s in range(CAP):
        at = jnp.maximum(codes[s], 0)
        pick = one_hot((COLS, BT * COLS), (at % BT) * COLS, COLS)
        rows = pl.ds(pl.multiple_of((at // BT) * ROWS, 16), ROWS)
        pieces.append(dot_nt(pick, rounded_ref[rows, :]).astype(BF)[:, 0:BLK])
    pieces.append(jnp.zeros((COLS, WIRE - META), BF))
    wire_ref[...] = jnp.concatenate(pieces, axis=1)


def all_codes(index_ref, count_ref):
    return [code_of(index_ref, count_ref, s) for s in range(CAP)]


def read_codes(panel_ref, note_ref, code_ref, sem):
    for k in range(TILES):
        note_ref[k:k + 1, :] = panel_ref[k, 0:16, TAIL:][0:1].astype(F32).astype(jnp.int32)
    copy = pltpu.make_async_copy(note_ref, code_ref, sem)
    copy.start()
    copy.wait()


def local_kernel(panel_ref, *refs):
    ham_refs, right_refs, (own_note, note_ref, code_ref, sem) = refs[0:4], refs[4:8], refs[8:]
    layer = lax.axis_index("layer")
    read_codes(panel_ref, note_ref, code_ref, sem)
    own_note[...] = note_ref[...]

    @pl.when(layer == 0)
    def _():
        for g in range(BT):
            unpack_right(code_ref, 0, g, panel_ref, right_refs[g])

    @pl.when(layer == 1)
    def _():
        for g in range(BT):
            unpack_ham(code_ref, g, panel_ref, ham_refs[g])


def first_kernel(index_ref, count_ref, other_ref, own_note, *refs):
    ham_refs, right_refs, (code_out, term_ref, out_ref) = refs[8:12], refs[12:16], refs[16:19]
    total_ref, rounded_ref, note_ref, code_ref, sem = refs[19:]
    layer = lax.axis_index("layer")
    read_codes(other_ref, note_ref, code_ref, sem)
    code_out[...] = jnp.where(layer == 0, own_note[...], note_ref[...])

    def pipelined(unpack):
        total = jnp.zeros((BT * ROWS, BT * COLS), F32)
        unpack(0)
        for g in range(BT):
            total = multiply(total, ham_refs[g], right_refs[g])
            if g + 1 < BT:
                unpack(g + 1)
        total_ref[...] = total

    @pl.when(layer == 0)
    def _():
        pipelined(lambda g: unpack_ham(code_ref, g, other_ref, ham_refs[g]))

    @pl.when(layer == 1)
    def _():
        pipelined(lambda g: unpack_right(code_ref, 0, g, other_ref, right_refs[g], COLS))

    codes = all_codes(index_ref, count_ref)
    term = keep(codes, total_ref[...])
    term_ref[...] = term
    pack(codes, term, rounded_ref, out_ref)


def second_kernel(code_ref, index_ref, count_ref, h0, h1, h2, h3, wire_ref, dense_ref, real_ref,
                  out_ref, r0, r1, r2, r3, rounded_ref):
    codes = all_codes(index_ref, count_ref)
    term = keep(codes, product((h0, h1, h2, h3), code_ref, 1, wire_ref, (r0, r1, r2, r3)))
    real_ref[...] = dense_ref[...] - 0.5 * term
    pack(codes, term, rounded_ref, out_ref)


def third_kernel(code_ref, index_ref, count_ref, h0, h1, h2, h3, wire_ref, first_ref, real_ref,
                 halves_ref, r0, r1, r2, r3):
    codes = all_codes(index_ref, count_ref)
    term = keep(codes, product((h0, h1, h2, h3), code_ref, 2, wire_ref, (r0, r1, r2, r3)))
    rows = BT * ROWS
    real, imag = real_ref[...], term / 6.0 - first_ref[...]
    halves_ref[0:rows] = real[:, 0:LANES]
    halves_ref[rows:2 * rows] = imag[:, 0:LANES]
    halves_ref[2 * rows:3 * rows] = jnp.concatenate([real[:, LANES:], imag[:, LANES:]], axis=1)


def join_kernel(own_ref, other_ref, *out_refs):
    swap = lax.axis_index("layer") == 1
    rows, rest = BT * ROWS, BT * COLS - LANES
    for n, out_ref in enumerate(out_refs):
        own, other = (
            jnp.concatenate(
                [ref[n * rows:(n + 1) * rows], ref[2 * rows:3 * rows][:, n * rest:(n + 1) * rest]],
                axis=1,
            )
            for ref in (own_ref, other_ref)
        )
        low, high = jnp.where(swap, other, own), jnp.where(swap, own, other)
        pieces = []
        for j in range(BT):
            pieces += [low[:, j * COLS:j * COLS + HALF], high[:, j * COLS:j * COLS + HALF]]
        whole = jnp.concatenate(pieces, axis=1)
        for i in range(BT):
            out_ref[i * BLK:(i + 1) * BLK, :] = whole[i * ROWS:i * ROWS + BLK, :]


def own_place(by_layer):
    high = lax.axis_index("y_lo") // 2
    if by_layer:
        high = jnp.where(lax.axis_index("layer") == 0, high, lax.axis_index("y_hi"))
    return high


def own_kernel(piece_ref, out_ref):
    at, piece = own_place(True), piece_ref[...]
    for n in range(out_ref.shape[0]):
        out_ref[n, at] = piece


def far_kernel(far_ref, pairs_ref, out_ref):
    del pairs_ref
    at, far = 1 - own_place(True), far_ref[...]
    for n in range(out_ref.shape[0]):
        out_ref[n, at] = far


def lay_kernel(piece_ref, far_ref, *refs):
    out_ref = refs[-1]
    at, piece, far = own_place(False), piece_ref[...], far_ref[...]
    for n in range(out_ref.shape[0]):
        out_ref[n, at] = piece
        out_ref[n, 1 - at] = far


def call(kernel, in_specs, arrays, out_shape, scratch=(), alias=None, vmem=24 << 20):
    return pl.pallas_call(
        kernel,
        out_shape=out_shape,
        in_specs=in_specs,
        out_specs=jax.tree.map(lambda _: VMEM, out_shape),
        input_output_aliases=alias or {},
        scratch_shapes=list(scratch),
        compiler_params=pltpu.CompilerParams(vmem_limit_bytes=vmem),
    )(*arrays)


def shape(*dims, dtype=BF):
    return jax.ShapeDtypeStruct(dims, dtype)


def place(x, y_lo, z, y_hi, layer):
    return (((x * 4 + y_lo) * 8 + z) * 2 + y_hi) * 2 + layer


def everywhere():
    return list(itertools.product(range(4), range(4), range(8), range(2), range(2)))


def pair_route(both):
    route = []
    for x, y_lo, z, y_hi, layer in everywhere():
        to = (x, y_lo, z, 1 - y_hi, layer) if both and layer else (x, y_lo ^ 2, z, y_hi, layer)
        route.append((place(x, y_lo, z, y_hi, layer), place(*to)))
    return route


def groups(both):
    found = {}
    for x, y_lo, z, y_hi, layer in everywhere():
        key = (layer, x, y_lo, y_hi) if both and layer else (layer, y_lo // 2, z, y_hi)
        found.setdefault(key, []).append(place(x, y_lo, z, y_hi, layer))
    return sorted(found.values())


def to_pair(piece, both):
    return lax.ppermute(piece, AXES, pair_route(both))


def spread(pairs, both):
    tiles = lax.all_to_all(pairs, AXES, 0, 0, axis_index_groups=groups(both))
    return tiles.reshape((TILES,) + tiles.shape[2:])


def swap(values):
    return lax.ppermute(values, "layer", [(0, 1), (1, 0)])


def per_device(ham_blocks, ham_index, ham_count, dens_blocks, dens_index, dens_count, first_index,
               first_count, second_index, second_count, third_index, third_count):
    index = pltpu.SMEM((2, 1, CAP), jnp.int32)
    packed = pltpu.VMEM((BLK, META), BF)
    payload = call(
        prep_kernel,
        [HBM, SMEM] * 4 + [HBM, HBM],
        (ham_index, ham_count, dens_index, dens_count, first_index, first_count, second_index,
         second_count, ham_blocks, dens_blocks),
        shape(ROWS, WIRE),
        [index] * 4 + [packed, packed, pltpu.SemaphoreType.DMA((6,))],
        vmem=62900000,
    )
    half = shape(BT * ROWS, BT * COLS, dtype=F32)
    pairs = call(own_kernel, [VMEM], (payload,), shape(8, 2, ROWS, WIRE))
    pairs = call(
        far_kernel, [VMEM] * 2, (to_pair(payload, True), pairs), shape(8, 2, ROWS, WIRE),
        alias={1: 0},
    )
    panel = spread(pairs, True)
    dense_ham = shape(BT + 1, BT * ROWS, BT * LANES)
    dense_right = [pltpu.VMEM((BT + 1, BT * COLS, BT * LANES), BF)] * BT
    rounded = pltpu.VMEM((BT * ROWS, BT * COLS), BF)
    code = pltpu.SMEM((TILES, LANES), jnp.int32)
    wire, wires = shape(COLS, WIRE), shape(8, 2, COLS, WIRE)
    note = shape(TILES, LANES, dtype=jnp.int32)
    reading = [pltpu.VMEM((TILES, LANES), jnp.int32), code, pltpu.SemaphoreType.DMA]
    made = (dense_ham,) * BT + (shape(BT + 1, BT * COLS, BT * LANES),) * BT
    *unpacked, own_note = call(local_kernel, [VMEM], (panel,), made + (note,), reading)
    out = call(
        first_kernel,
        [SMEM] * 2 + [VMEM] * 10,
        (first_index, first_count, swap(panel), own_note, *unpacked),
        made + (note, half, wire),
        [pltpu.VMEM((BT * ROWS, BT * COLS), F32), rounded] + reading,
        alias={4 + n: n for n in range(8)},
    )
    ham, (codes, first_term, first_wire) = out[0:4], out[8:]
    dense_half = call(
        dense_kernel, [SMEM, SMEM, VMEM, VMEM], (dens_index, dens_count, dens_blocks, codes), half
    )
    pairs = call(
        lay_kernel,
        [VMEM] * 3,
        (first_wire, to_pair(first_wire, False), dense_half),
        wires,
    )
    real_half, second_wire = call(
        second_kernel,
        [SMEM] * 3 + [VMEM] * 6,
        (codes, second_index, second_count, *ham, spread(pairs, False), dense_half),
        (half, wire),
        dense_right + [rounded],
    )
    pairs = call(
        lay_kernel,
        [VMEM, VMEM, SMEM],
        (second_wire, to_pair(second_wire, False), third_count),
        wires,
    )
    halves = call(
        third_kernel,
        [SMEM] * 3 + [VMEM] * 7,
        (codes, third_index, third_count, *ham, spread(pairs, False), first_term, real_half),
        shape(3 * BT * ROWS, LANES, dtype=F32),
        dense_right,
    )
    whole = shape(SIDE, SIDE, dtype=F32)
    return call(join_kernel, [VMEM] * 2, (halves, swap(halves)), (whole, whole))


def solution(mesh):
    split = Mesh(mesh.devices.reshape(4, 4, 8, 2, 2), AXES)
    row, col = ("x", "y_lo"), ("z", "y_hi")
    blocks, index = P(row, col), P(None, row, col)
    in_specs = (blocks, index, blocks) * 2 + (index, blocks) * 3
    return jax.shard_map(
        per_device, mesh=split, in_specs=in_specs, out_specs=(blocks, blocks), check_vma=False
    )
```

```python
import itertools

import jax
import jax.numpy as jnp
from jax import lax
from jax.experimental import pallas as pl
from jax.experimental.pallas import tpu as pltpu
from jax.sharding import Mesh, PartitionSpec as P

BLK = 92
HALF = 46
BT = 4
CAP = 8
ROWS = 96
COLS = 48
LANES = 128
SIDE = BT * BLK
WIRE = 768
META = 736
TAIL = WIRE - LANES
TILES = 16
AXES = ("x", "y_lo", "z", "y_hi", "layer")
BF = jnp.bfloat16
F32 = jnp.float32
VMEM = pl.BlockSpec(memory_space=pltpu.VMEM)
SMEM = pl.BlockSpec(memory_space=pltpu.SMEM)
HBM = pl.BlockSpec(memory_space=pltpu.HBM)


def dot_nt(a, b):
    return lax.dot_general(a, b, (((1,), (1,)), ((), ())), preferred_element_type=F32)


def one_hot(shape, shift, width):
    q = lax.broadcasted_iota(jnp.int32, shape, 0)
    x = lax.broadcasted_iota(jnp.int32, shape, 1)
    return jnp.where((x == q + shift) & (q < width), 1.0, 0.0).astype(BF)


def code_of(index_ref, count_ref, s):
    return jnp.where(s < count_ref[0, 0], index_ref[0, 0, s] * BT + index_ref[1, 0, s], -1)


def prep_kernel(hidx_hbm, hcnt_ref, didx_hbm, dcnt_ref, fidx_hbm, fcnt_ref, sidx_hbm, scnt_ref,
                ham_hbm, dens_hbm, out_ref, hidx_ref, didx_ref, fidx_ref, sidx_ref, ham_ref,
                dens_ref, sems):
    pairs = ((ham_hbm, ham_ref), (dens_hbm, dens_ref), (hidx_hbm, hidx_ref), (didx_hbm, didx_ref),
             (fidx_hbm, fidx_ref), (sidx_hbm, sidx_ref))
    copies = [pltpu.make_async_copy(src, dst, sems.at[n]) for n, (src, dst) in enumerate(pairs)]
    for one in copies:
        one.start()
    for one in copies:
        one.wait()
    layer = lax.axis_index("layer")
    lane = lax.broadcasted_iota(jnp.int32, (ROWS, LANES), 1) - (META - TAIL)

    def noted(tail, *lists):
        for n, (index_ref, count_ref) in enumerate(lists):
            for s in range(CAP):
                code = code_of(index_ref, count_ref, s).astype(F32)
                tail = jnp.where(lane == n * CAP + s, code, tail)
        return tail.astype(BF)

    @pl.when(layer == 0)
    def _():
        dens = dens_ref[...]
        r = lax.broadcasted_iota(jnp.int32, (2 * COLS, META), 0)
        x = lax.broadcasted_iota(jnp.int32, (2 * COLS, META), 1)
        q = r % COLS
        pieces = []
        for s in range(CAP):
            pick = (x == q + (r // COLS) * HALF + s * BLK) & (q < HALF)
            pieces.append(dot_nt(jnp.where(pick, 1.0, 0.0).astype(BF), dens))
        pieces.append(jnp.zeros((2 * COLS, WIRE - META), F32))
        wire = jnp.concatenate(pieces, axis=1)
        out_ref[:, 0:TAIL] = wire[:, 0:TAIL].astype(BF)
        out_ref[:, TAIL:] = noted(
            wire[:, TAIL:], (didx_ref, dcnt_ref), (fidx_ref, fcnt_ref), (sidx_ref, scnt_ref)
        )

    @pl.when(layer == 1)
    def _():
        out_ref[...] = jnp.zeros_like(out_ref)
        out_ref[0:BLK, 0:META] = ham_ref[...]
        tail = out_ref[:, TAIL:].astype(F32)
        out_ref[:, TAIL:] = noted(tail, (hidx_ref, hcnt_ref))


def dense_kernel(didx_ref, dcnt_ref, dens_ref, after_ref, dense_ref):
    del after_ref
    layer = lax.axis_index("layer")
    dens = dens_ref[...]
    dense_ref[...] = jnp.zeros_like(dense_ref)
    for s in range(CAP):
        code = code_of(didx_ref, dcnt_ref, s)
        at = jnp.maximum(code, 0)
        i, j = at // BT, at % BT
        x = lax.broadcasted_iota(jnp.int32, (META, BT * COLS), 0)
        y = lax.broadcasted_iota(jnp.int32, (META, BT * COLS), 1) - j * COLS
        spread = jnp.where(
            (x == y + (s * BLK + layer * HALF)) & (y >= 0) & (y < HALF) & (code >= 0), 1.0, 0.0
        ).astype(BF)
        block = jnp.dot(dens, spread, preferred_element_type=F32)
        block = jnp.concatenate([block, jnp.zeros((ROWS - BLK, BT * COLS), F32)], axis=0)
        rows = pl.ds(pl.multiple_of(i * ROWS, ROWS), ROWS)
        dense_ref[rows, :] = dense_ref[rows, :] + block


def unpack_ham(code_ref, g, from_ref, ham_ref):
    for t in range(BT):
        wire = from_ref[g * BT + t]
        for s in range(CAP):
            code = code_ref[g * BT + t, META - TAIL + s]
            at = jnp.maximum(code, 0)
            where = jnp.where(code >= 0, t, BT)
            rows = pl.ds(pl.multiple_of((at // BT) * ROWS, 16), ROWS)
            lanes = pl.ds(pl.multiple_of((at % BT) * LANES, LANES), BLK)
            ham_ref[where, rows, lanes] = wire[:, s * BLK:(s + 1) * BLK]


def unpack_right(code_ref, which, wire_ref, order, right_ref, first_row=0):
    for t, n in enumerate(order):
        wire = wire_ref[n, pl.ds(first_row, COLS), :]
        for s in range(CAP):
            code = code_ref[n, META - TAIL + which * CAP + s]
            at = jnp.maximum(code, 0)
            where = jnp.where(code >= 0, t, BT)
            rows = pl.ds(pl.multiple_of((at % BT) * COLS, 16), COLS)
            lanes = pl.ds(pl.multiple_of((at // BT) * LANES, LANES), BLK)
            right_ref[where, rows, lanes] = wire[:, s * BLK:(s + 1) * BLK]


def dens_order(g):
    return [g // 2 * 8 + y_lo * 2 + g % 2 for y_lo in range(BT)]


def term_order(g):
    return [g * BT + y_lo % 2 * 2 + y_lo // 2 for y_lo in range(BT)]


def multiply(total, ham_ref, right_ref):
    for t in range(BT):
        total = total + dot_nt(ham_ref[t], right_ref[t])
    return total


def product(ham_refs, code_ref, which, wire_ref, right_refs):
    total = jnp.zeros((BT * ROWS, BT * COLS), F32)
    right_refs[0][...] = jnp.zeros_like(right_refs[0])
    unpack_right(code_ref, which, wire_ref, term_order(0), right_refs[0])
    for g in range(BT):
        total = multiply(total, ham_refs[g], right_refs[g])
        if g + 1 < BT:
            right_refs[g + 1][...] = jnp.zeros_like(right_refs[g + 1])
            unpack_right(code_ref, which, wire_ref, term_order(g + 1), right_refs[g + 1])
    return total


def keep(codes, total):
    row = lax.broadcasted_iota(jnp.int32, total.shape, 0) // ROWS
    col = lax.broadcasted_iota(jnp.int32, total.shape, 1) // COLS
    place = row * BT + col
    kept = place == codes[0]
    for s in range(1, CAP):
        kept = kept | (place == codes[s])
    return jnp.where(kept, total, 0.0)


def pack(codes, term, rounded_ref, wire_ref):
    rounded_ref[...] = term.astype(BF)
    pieces = []
    for s in range(CAP):
        at = jnp.maximum(codes[s], 0)
        pick = one_hot((COLS, BT * COLS), (at % BT) * COLS, COLS)
        rows = pl.ds(pl.multiple_of((at // BT) * ROWS, 16), ROWS)
        pieces.append(dot_nt(pick, rounded_ref[rows, :]).astype(BF)[:, 0:BLK])
    pieces.append(jnp.zeros((COLS, WIRE - META), BF))
    wire_ref[...] = jnp.concatenate(pieces, axis=1)


def all_codes(index_ref, count_ref):
    return [code_of(index_ref, count_ref, s) for s in range(CAP)]


def read_codes(panel_ref, note_ref, code_ref, sem):
    for k in range(TILES):
        note_ref[k:k + 1, :] = panel_ref[k, 0:16, TAIL:][0:1].astype(F32).astype(jnp.int32)
    copy = pltpu.make_async_copy(note_ref, code_ref, sem)
    copy.start()
    copy.wait()


def local_kernel(panel_ref, *refs):
    ham_refs, right_refs, (own_note, note_ref, code_ref, sem) = refs[0:4], refs[4:8], refs[8:]
    layer = lax.axis_index("layer")
    read_codes(panel_ref, note_ref, code_ref, sem)
    own_note[...] = note_ref[...]
    for ref in (*ham_refs, *right_refs):
        ref[...] = jnp.zeros_like(ref)

    @pl.when(layer == 0)
    def _():
        for g in range(BT):
            unpack_right(code_ref, 0, panel_ref, dens_order(g), right_refs[g])

    @pl.when(layer == 1)
    def _():
        for g in range(BT):
            unpack_ham(code_ref, g, panel_ref, ham_refs[g])


def first_kernel(index_ref, count_ref, other_ref, own_note, *refs):
    ham_refs, right_refs, (code_out, term_ref, out_ref) = refs[8:12], refs[12:16], refs[16:19]
    total_ref, rounded_ref, note_ref, code_ref, sem = refs[19:]
    layer = lax.axis_index("layer")
    read_codes(other_ref, note_ref, code_ref, sem)
    for g in range(BT):
        for n, to in zip(dens_order(g), term_order(g)):
            code_out[to:to + 1, :] = jnp.where(layer == 0, own_note[n:n + 1, :], note_ref[n:n + 1, :])

    def pipelined(unpack):
        total = jnp.zeros((BT * ROWS, BT * COLS), F32)
        unpack(0)
        for g in range(BT):
            total = multiply(total, ham_refs[g], right_refs[g])
            if g + 1 < BT:
                unpack(g + 1)
        total_ref[...] = total

    @pl.when(layer == 0)
    def _():
        pipelined(lambda g: unpack_ham(code_ref, g, other_ref, ham_refs[g]))

    @pl.when(layer == 1)
    def _():
        pipelined(lambda g: unpack_right(code_ref, 0, other_ref, dens_order(g), right_refs[g], COLS))

    codes = all_codes(index_ref, count_ref)
    term = keep(codes, total_ref[...])
    term_ref[...] = term
    pack(codes, term, rounded_ref, out_ref)


def second_kernel(code_ref, index_ref, count_ref, h0, h1, h2, h3, wire_ref, dense_ref, real_ref,
                  out_ref, r0, r1, r2, r3, rounded_ref):
    codes = all_codes(index_ref, count_ref)
    term = keep(codes, product((h0, h1, h2, h3), code_ref, 1, wire_ref, (r0, r1, r2, r3)))
    real_ref[...] = dense_ref[...] - 0.5 * term
    pack(codes, term, rounded_ref, out_ref)


def third_kernel(code_ref, index_ref, count_ref, h0, h1, h2, h3, wire_ref, first_ref, real_ref,
                 halves_ref, r0, r1, r2, r3):
    codes = all_codes(index_ref, count_ref)
    term = keep(codes, product((h0, h1, h2, h3), code_ref, 2, wire_ref, (r0, r1, r2, r3)))
    rows = BT * ROWS
    real, imag = real_ref[...], term / 6.0 - first_ref[...]
    halves_ref[0:rows] = real[:, 0:LANES]
    halves_ref[rows:2 * rows] = imag[:, 0:LANES]
    halves_ref[2 * rows:3 * rows] = jnp.concatenate([real[:, LANES:], imag[:, LANES:]], axis=1)


def put_half(from_ref, n, layer, out_ref, add):
    rows, rest = BT * ROWS, BT * COLS - LANES
    half = jnp.concatenate(
        [from_ref[n * rows:(n + 1) * rows], from_ref[2 * rows:3 * rows][:, n * rest:(n + 1) * rest]],
        axis=1,
    )
    gap = jnp.zeros((rows, HALF), F32)
    pieces = []
    for j in range(BT):
        piece = half[:, j * COLS:j * COLS + HALF]
        pieces += [gap, piece] if layer else [piece, gap]
    whole = jnp.concatenate(pieces, axis=1)
    for i in range(BT):
        to = slice(i * BLK, (i + 1) * BLK)
        block = whole[i * ROWS:i * ROWS + BLK, :]
        out_ref[to, :] = add[to, :] + block if add is not None else block


def own_half_kernel(own_ref, *out_refs):
    for layer in range(2):
        @pl.when(lax.axis_index("layer") == layer)
        def _(layer=layer):
            for n, out_ref in enumerate(out_refs):
                put_half(own_ref, n, layer, out_ref, None)


def other_half_kernel(other_ref, real_ref, imag_ref, *out_refs):
    for layer in range(2):
        @pl.when(lax.axis_index("layer") == layer)
        def _(layer=layer):
            for n, out_ref in enumerate(out_refs):
                put_half(other_ref, n, 1 - layer, out_ref, (real_ref, imag_ref)[n])


def own_place(by_layer):
    if by_layer:
        return jnp.where(lax.axis_index("layer") == 0, lax.axis_index("x") % 2, lax.axis_index("y_hi"))
    return lax.axis_index("y_lo") // 2


def own_kernel(piece_ref, out_ref):
    at, piece = own_place(True), piece_ref[...]
    for n in range(out_ref.shape[0]):
        out_ref[n, at] = piece


def far_kernel(far_ref, pairs_ref, out_ref):
    del pairs_ref
    at, far = 1 - own_place(True), far_ref[...]
    for n in range(out_ref.shape[0]):
        out_ref[n, at] = far


def lay_kernel(piece_ref, far_ref, *refs):
    out_ref = refs[-1]
    at, piece, far = own_place(False), piece_ref[...], far_ref[...]
    for n in range(out_ref.shape[0]):
        out_ref[n, at] = piece
        out_ref[n, 1 - at] = far


def call(kernel, in_specs, arrays, out_shape, scratch=(), alias=None, vmem=24 << 20):
    return pl.pallas_call(
        kernel,
        out_shape=out_shape,
        in_specs=in_specs,
        out_specs=jax.tree.map(lambda _: VMEM, out_shape),
        input_output_aliases=alias or {},
        scratch_shapes=list(scratch),
        compiler_params=pltpu.CompilerParams(vmem_limit_bytes=vmem),
    )(*arrays)


def shape(*dims, dtype=BF):
    return jax.ShapeDtypeStruct(dims, dtype)


def place(x, y_lo, z, y_hi, layer):
    return (((x * 4 + y_lo) * 8 + z) * 2 + y_hi) * 2 + layer


def everywhere():
    return list(itertools.product(range(4), range(4), range(8), range(2), range(2)))


def pair_route(both):
    route = []
    for x, y_lo, z, y_hi, layer in everywhere():
        to = (x, y_lo ^ 2, z, y_hi, layer)
        if both:
            to = (x, y_lo, z, 1 - y_hi, layer) if layer else (x ^ 1, y_lo, z, y_hi, layer)
        route.append((place(x, y_lo, z, y_hi, layer), place(*to)))
    return route


def groups(both):
    found = {}
    for x, y_lo, z, y_hi, layer in everywhere():
        key = (layer, y_lo // 2, z, y_hi)
        if both:
            key = (layer, x, y_lo, y_hi) if layer else (layer, x % 2, z, y_hi)
        found.setdefault(key, []).append(place(x, y_lo, z, y_hi, layer))
    return sorted(found.values())


def to_pair(piece, both):
    return lax.ppermute(piece, AXES, pair_route(both))


def spread(pairs, both):
    tiles = lax.all_to_all(pairs, AXES, 0, 0, axis_index_groups=groups(both))
    return tiles.reshape((TILES,) + tiles.shape[2:])


def swap(values):
    return lax.ppermute(values, "layer", [(0, 1), (1, 0)])


def per_device(ham_blocks, ham_index, ham_count, dens_blocks, dens_index, dens_count, first_index,
               first_count, second_index, second_count, third_index, third_count):
    index = pltpu.SMEM((2, 1, CAP), jnp.int32)
    packed = pltpu.VMEM((BLK, META), BF)
    payload = call(
        prep_kernel,
        [HBM, SMEM] * 4 + [HBM, HBM],
        (ham_index, ham_count, dens_index, dens_count, first_index, first_count, second_index,
         second_count, ham_blocks, dens_blocks),
        shape(ROWS, WIRE),
        [index] * 4 + [packed, packed, pltpu.SemaphoreType.DMA((6,))],
        vmem=62900000,
    )
    half = shape(BT * ROWS, BT * COLS, dtype=F32)
    pairs = call(own_kernel, [VMEM], (payload,), shape(8, 2, ROWS, WIRE))
    pairs = call(
        far_kernel, [VMEM] * 2, (to_pair(payload, True), pairs), shape(8, 2, ROWS, WIRE),
        alias={1: 0},
    )
    panel = spread(pairs, True)
    dense_ham = shape(BT + 1, BT * ROWS, BT * LANES)
    dense_right = [pltpu.VMEM((BT + 1, BT * COLS, BT * LANES), BF)] * BT
    rounded = pltpu.VMEM((BT * ROWS, BT * COLS), BF)
    code = pltpu.SMEM((TILES, LANES), jnp.int32)
    wire, wires = shape(COLS, WIRE), shape(8, 2, COLS, WIRE)
    note = shape(TILES, LANES, dtype=jnp.int32)
    reading = [pltpu.VMEM((TILES, LANES), jnp.int32), code, pltpu.SemaphoreType.DMA]
    made = (dense_ham,) * BT + (shape(BT + 1, BT * COLS, BT * LANES),) * BT
    *unpacked, own_note = call(local_kernel, [VMEM], (panel,), made + (note,), reading)
    out = call(
        first_kernel,
        [SMEM] * 2 + [VMEM] * 10,
        (first_index, first_count, swap(panel), own_note, *unpacked),
        made + (note, half, wire),
        [pltpu.VMEM((BT * ROWS, BT * COLS), F32), rounded] + reading,
        alias={4 + n: n for n in range(8)},
    )
    ham, (codes, first_term, first_wire) = out[0:4], out[8:]
    dense_half = call(
        dense_kernel, [SMEM, SMEM, VMEM, VMEM], (dens_index, dens_count, dens_blocks, codes), half
    )
    pairs = call(
        lay_kernel,
        [VMEM] * 3,
        (first_wire, to_pair(first_wire, False), dense_half),
        wires,
    )
    real_half, second_wire = call(
        second_kernel,
        [SMEM] * 3 + [VMEM] * 6,
        (codes, second_index, second_count, *ham, spread(pairs, False), dense_half),
        (half, wire),
        dense_right + [rounded],
    )
    pairs = call(
        lay_kernel,
        [VMEM, VMEM, SMEM],
        (second_wire, to_pair(second_wire, False), third_count),
        wires,
    )
    halves = call(
        third_kernel,
        [SMEM] * 3 + [VMEM] * 7,
        (codes, third_index, third_count, *ham, spread(pairs, False), first_term, real_half),
        shape(3 * BT * ROWS, LANES, dtype=F32),
        dense_right,
    )
    whole = shape(SIDE, SIDE, dtype=F32)
    own = call(own_half_kernel, [VMEM], (halves,), (whole, whole))
    return call(other_half_kernel, [VMEM] * 3, (swap(halves), *own), (whole, whole))


def solution(mesh):
    split = Mesh(mesh.devices.reshape(4, 4, 8, 2, 2), AXES)
    row, col = ("x", "y_lo"), ("z", "y_hi")
    blocks, index = P(row, col), P(None, row, col)
    in_specs = (blocks, index, blocks) * 2 + (index, blocks) * 3
    return jax.shard_map(
        per_device, mesh=split, in_specs=in_specs, out_specs=(blocks, blocks), check_vma=False
    )
```

```python
import itertools

import jax
import jax.numpy as jnp
from jax import lax
from jax.experimental import pallas as pl
from jax.experimental.pallas import tpu as pltpu
from jax.sharding import Mesh, PartitionSpec as P

BLK = 92
HALF = 46
BT = 4
CAP = 8
ROWS = 96
COLS = 48
LANES = 128
SIDE = BT * BLK
WIRE = 768
META = 736
CODES = 464
WROWS = WIRE // LANES * BLK
TAIL = WIRE - LANES
TILES = 16
AXES = ("x", "y_lo", "z", "y_hi", "layer")
BF = jnp.bfloat16
F32 = jnp.float32
VMEM = pl.BlockSpec(memory_space=pltpu.VMEM)
SMEM = pl.BlockSpec(memory_space=pltpu.SMEM)
HBM = pl.BlockSpec(memory_space=pltpu.HBM)


def dot_nt(a, b):
    return lax.dot_general(a, b, (((1,), (1,)), ((), ())), preferred_element_type=F32)


def one_hot(shape, shift, width):
    q = lax.broadcasted_iota(jnp.int32, shape, 0)
    x = lax.broadcasted_iota(jnp.int32, shape, 1)
    return jnp.where((x == q + shift) & (q < width), 1.0, 0.0).astype(BF)


def code_of(index_ref, count_ref, s):
    return jnp.where(s < count_ref[0, 0], index_ref[0, 0, s] * BT + index_ref[1, 0, s], -1)


def prep_kernel(hidx_hbm, hcnt_ref, didx_hbm, dcnt_ref, fidx_hbm, fcnt_ref, sidx_hbm, scnt_ref,
                ham_hbm, dens_hbm, out_ref, hidx_ref, didx_ref, fidx_ref, sidx_ref, ham_ref,
                dens_ref, sems):
    pairs = ((ham_hbm, ham_ref), (dens_hbm, dens_ref), (hidx_hbm, hidx_ref), (didx_hbm, didx_ref),
             (fidx_hbm, fidx_ref), (sidx_hbm, sidx_ref))
    copies = [pltpu.make_async_copy(src, dst, sems.at[n]) for n, (src, dst) in enumerate(pairs)]
    for one in copies:
        one.start()
    for one in copies:
        one.wait()
    layer = lax.axis_index("layer")
    lane = lax.broadcasted_iota(jnp.int32, (BLK, LANES), 1) - (META - TAIL)

    def store(wire, *lists):
        tail = wire[:, TAIL:]
        for n, (index_ref, count_ref) in enumerate(lists):
            for s in range(CAP):
                tail = jnp.where(lane == n * CAP + s, code_of(index_ref, count_ref, s).astype(F32), tail)
        for t in range(TAIL // LANES):
            out_ref[t * BLK:(t + 1) * BLK, :] = wire[:, t * LANES:(t + 1) * LANES].astype(BF)
        out_ref[WROWS - BLK:, :] = tail.astype(BF)

    @pl.when(layer == 0)
    def _():
        dens = dens_ref[...]
        pieces = [dot_nt(one_hot((BLK, META), s * BLK, BLK), dens) for s in range(CAP)]
        store(
            jnp.concatenate(pieces + [jnp.zeros((BLK, WIRE - META), F32)], axis=1),
            (didx_ref, dcnt_ref), (fidx_ref, fcnt_ref), (sidx_ref, scnt_ref),
        )

    @pl.when(layer == 1)
    def _():
        wire = jnp.concatenate([ham_ref[...].astype(F32), jnp.zeros((BLK, WIRE - META), F32)], axis=1)
        store(wire, (hidx_ref, hcnt_ref))


def dense_kernel(didx_ref, dcnt_ref, dens_ref, after_ref, dense_ref):
    del after_ref
    layer = lax.axis_index("layer")
    dens = dens_ref[...]
    dense_ref[...] = jnp.zeros_like(dense_ref)
    for s in range(CAP):
        code = code_of(didx_ref, dcnt_ref, s)
        at = jnp.maximum(code, 0)
        i, j = at // BT, at % BT
        x = lax.broadcasted_iota(jnp.int32, (META, BT * COLS), 0)
        y = lax.broadcasted_iota(jnp.int32, (META, BT * COLS), 1) - j * COLS
        spread = jnp.where(
            (x == y + (s * BLK + layer * HALF)) & (y >= 0) & (y < HALF) & (code >= 0), 1.0, 0.0
        ).astype(BF)
        block = jnp.dot(dens, spread, preferred_element_type=F32)
        block = jnp.concatenate([block, jnp.zeros((ROWS - BLK, BT * COLS), F32)], axis=0)
        rows = pl.ds(pl.multiple_of(i * ROWS, ROWS), ROWS)
        dense_ref[rows, :] = dense_ref[rows, :] + block


def piece_rows(from_ref, n, first, rows):
    at = [t * BLK + first for t in range(WIRE // LANES)]
    return jnp.concatenate([from_ref[n, row:row + rows, :] for row in at], axis=1)


def unpack_ham(code_ref, g, from_ref, ham_ref):
    for t in range(BT):
        wire = piece_rows(from_ref, g * BT + t, 0, BLK)
        for s in range(CAP):
            code = code_ref[g * BT + t, META - TAIL + s]
            at = jnp.maximum(code, 0)
            where = jnp.where(code >= 0, t, BT)
            rows = pl.ds(pl.multiple_of((at // BT) * ROWS, 16), BLK)
            lanes = pl.ds(pl.multiple_of((at % BT) * LANES, LANES), BLK)
            ham_ref[where, rows, lanes] = wire[:, s * BLK:(s + 1) * BLK]


def unpack_dens(code_ref, g, from_ref, half, right_ref):
    for t, n in enumerate(dens_order(g)):
        wire = piece_rows(from_ref, n, half * HALF, HALF)
        for s in range(CAP):
            code = code_ref[n, META - TAIL + s]
            at = jnp.maximum(code, 0)
            where = jnp.where(code >= 0, t, BT)
            rows = pl.ds(pl.multiple_of((at % BT) * COLS, 16), HALF)
            lanes = pl.ds(pl.multiple_of((at // BT) * LANES, LANES), BLK)
            right_ref[where, rows, lanes] = wire[:, s * BLK:(s + 1) * BLK]


def unpack_right(code_ref, which, wire_ref, order, right_ref, first_row=0):
    for t, n in enumerate(order):
        wire = wire_ref[n, pl.ds(first_row, COLS), :]
        for s in range(CAP):
            code = code_ref[n, META - TAIL + which * CAP + s]
            at = jnp.maximum(code, 0)
            where = jnp.where(code >= 0, t, BT)
            rows = pl.ds(pl.multiple_of((at % BT) * COLS, 16), COLS)
            lanes = pl.ds(pl.multiple_of((at // BT) * LANES, LANES), BLK)
            right_ref[where, rows, lanes] = wire[:, s * BLK:(s + 1) * BLK]


def dens_order(g):
    return [g // 2 * 8 + y_lo * 2 + g % 2 for y_lo in range(BT)]


def term_order(g):
    return [g * BT + y_lo % 2 * 2 + y_lo // 2 for y_lo in range(BT)]


def multiply(total, ham_ref, right_ref):
    for t in range(BT):
        total = total + dot_nt(ham_ref[t], right_ref[t])
    return total


def product(ham_refs, code_ref, which, wire_ref, right_refs):
    total = jnp.zeros((BT * ROWS, BT * COLS), F32)
    right_refs[0][...] = jnp.zeros_like(right_refs[0])
    unpack_right(code_ref, which, wire_ref, term_order(0), right_refs[0])
    for g in range(BT):
        total = multiply(total, ham_refs[g], right_refs[g])
        if g + 1 < BT:
            right_refs[g + 1][...] = jnp.zeros_like(right_refs[g + 1])
            unpack_right(code_ref, which, wire_ref, term_order(g + 1), right_refs[g + 1])
    return total


def keep(codes, total):
    row = lax.broadcasted_iota(jnp.int32, total.shape, 0) // ROWS
    col = lax.broadcasted_iota(jnp.int32, total.shape, 1) // COLS
    place = row * BT + col
    kept = place == codes[0]
    for s in range(1, CAP):
        kept = kept | (place == codes[s])
    return jnp.where(kept, total, 0.0)


def pack(codes, term, rounded_ref, wire_ref):
    rounded_ref[...] = term.astype(BF)
    pieces = []
    for s in range(CAP):
        at = jnp.maximum(codes[s], 0)
        pick = one_hot((COLS, BT * COLS), (at % BT) * COLS, COLS)
        rows = pl.ds(pl.multiple_of((at // BT) * ROWS, 16), ROWS)
        pieces.append(dot_nt(pick, rounded_ref[rows, :]).astype(BF)[:, 0:BLK])
    pieces.append(jnp.zeros((COLS, WIRE - META), BF))
    wire_ref[...] = jnp.concatenate(pieces, axis=1)


def all_codes(index_ref, count_ref):
    return [code_of(index_ref, count_ref, s) for s in range(CAP)]


def read_codes(panel_ref, note_ref, code_ref, sem):
    for k in range(TILES):
        note_ref[k:k + 1, :] = panel_ref[k, CODES:CODES + 16, :][0:1].astype(F32).astype(jnp.int32)
    copy = pltpu.make_async_copy(note_ref, code_ref, sem)
    copy.start()
    copy.wait()


def local_kernel(panel_ref, *refs):
    ham_refs, right_refs, (own_note, note_ref, code_ref, sem) = refs[0:4], refs[4:8], refs[8:]
    layer = lax.axis_index("layer")
    read_codes(panel_ref, note_ref, code_ref, sem)
    own_note[...] = note_ref[...]
    for ref in (*ham_refs, *right_refs):
        ref[...] = jnp.zeros_like(ref)

    @pl.when(layer == 0)
    def _():
        for g in range(BT):
            unpack_dens(code_ref, g, panel_ref, 0, right_refs[g])

    @pl.when(layer == 1)
    def _():
        for g in range(BT):
            unpack_ham(code_ref, g, panel_ref, ham_refs[g])


def first_kernel(index_ref, count_ref, other_ref, own_note, *refs):
    ham_refs, right_refs, (code_out, term_ref, out_ref) = refs[8:12], refs[12:16], refs[16:19]
    total_ref, rounded_ref, note_ref, code_ref, sem = refs[19:]
    layer = lax.axis_index("layer")
    read_codes(other_ref, note_ref, code_ref, sem)
    for g in range(BT):
        for n, to in zip(dens_order(g), term_order(g)):
            code_out[to:to + 1, :] = jnp.where(layer == 0, own_note[n:n + 1, :], note_ref[n:n + 1, :])

    def pipelined(unpack):
        total = jnp.zeros((BT * ROWS, BT * COLS), F32)
        unpack(0)
        for g in range(BT):
            total = multiply(total, ham_refs[g], right_refs[g])
            if g + 1 < BT:
                unpack(g + 1)
        total_ref[...] = total

    @pl.when(layer == 0)
    def _():
        pipelined(lambda g: unpack_ham(code_ref, g, other_ref, ham_refs[g]))

    @pl.when(layer == 1)
    def _():
        pipelined(lambda g: unpack_dens(code_ref, g, other_ref, 1, right_refs[g]))

    codes = all_codes(index_ref, count_ref)
    term = keep(codes, total_ref[...])
    term_ref[...] = term
    pack(codes, term, rounded_ref, out_ref)


def second_kernel(code_ref, index_ref, count_ref, h0, h1, h2, h3, wire_ref, dense_ref, real_ref,
                  out_ref, r0, r1, r2, r3, rounded_ref):
    codes = all_codes(index_ref, count_ref)
    term = keep(codes, product((h0, h1, h2, h3), code_ref, 1, wire_ref, (r0, r1, r2, r3)))
    real_ref[...] = dense_ref[...] - 0.5 * term
    pack(codes, term, rounded_ref, out_ref)


def third_kernel(code_ref, index_ref, count_ref, h0, h1, h2, h3, wire_ref, first_ref, real_ref,
                 halves_ref, r0, r1, r2, r3):
    codes = all_codes(index_ref, count_ref)
    term = keep(codes, product((h0, h1, h2, h3), code_ref, 2, wire_ref, (r0, r1, r2, r3)))
    rows = BT * ROWS
    real, imag = real_ref[...], term / 6.0 - first_ref[...]
    halves_ref[0:rows] = real[:, 0:LANES]
    halves_ref[rows:2 * rows] = imag[:, 0:LANES]
    halves_ref[2 * rows:3 * rows] = jnp.concatenate([real[:, LANES:], imag[:, LANES:]], axis=1)


def put_half(from_ref, n, layer, out_ref, add):
    rows, rest = BT * ROWS, BT * COLS - LANES
    half = jnp.concatenate(
        [from_ref[n * rows:(n + 1) * rows], from_ref[2 * rows:3 * rows][:, n * rest:(n + 1) * rest]],
        axis=1,
    )
    gap = jnp.zeros((rows, HALF), F32)
    pieces = []
    for j in range(BT):
        piece = half[:, j * COLS:j * COLS + HALF]
        pieces += [gap, piece] if layer else [piece, gap]
    whole = jnp.concatenate(pieces, axis=1)
    for i in range(BT):
        to = slice(i * BLK, (i + 1) * BLK)
        block = whole[i * ROWS:i * ROWS + BLK, :]
        out_ref[to, :] = add[to, :] + block if add is not None else block


def own_half_kernel(own_ref, *out_refs):
    for layer in range(2):
        @pl.when(lax.axis_index("layer") == layer)
        def _(layer=layer):
            for n, out_ref in enumerate(out_refs):
                put_half(own_ref, n, layer, out_ref, None)


def other_half_kernel(other_ref, real_ref, imag_ref, *out_refs):
    for layer in range(2):
        @pl.when(lax.axis_index("layer") == layer)
        def _(layer=layer):
            for n, out_ref in enumerate(out_refs):
                put_half(other_ref, n, 1 - layer, out_ref, (real_ref, imag_ref)[n])


def own_place(by_layer):
    if by_layer:
        return jnp.where(lax.axis_index("layer") == 0, lax.axis_index("x") % 2, lax.axis_index("y_hi"))
    return lax.axis_index("y_lo") // 2


def own_kernel(piece_ref, out_ref):
    at, piece = own_place(True), piece_ref[...]
    for n in range(out_ref.shape[0]):
        out_ref[n, at] = piece


def far_kernel(far_ref, pairs_ref, out_ref):
    del pairs_ref
    at, far = 1 - own_place(True), far_ref[...]
    for n in range(out_ref.shape[0]):
        out_ref[n, at] = far


def lay_kernel(piece_ref, far_ref, *refs):
    out_ref = refs[-1]
    at, piece, far = own_place(False), piece_ref[...], far_ref[...]
    for n in range(out_ref.shape[0]):
        out_ref[n, at] = piece
        out_ref[n, 1 - at] = far


def call(kernel, in_specs, arrays, out_shape, scratch=(), alias=None, vmem=24 << 20):
    return pl.pallas_call(
        kernel,
        out_shape=out_shape,
        in_specs=in_specs,
        out_specs=jax.tree.map(lambda _: VMEM, out_shape),
        input_output_aliases=alias or {},
        scratch_shapes=list(scratch),
        compiler_params=pltpu.CompilerParams(vmem_limit_bytes=vmem),
    )(*arrays)


def shape(*dims, dtype=BF):
    return jax.ShapeDtypeStruct(dims, dtype)


def place(x, y_lo, z, y_hi, layer):
    return (((x * 4 + y_lo) * 8 + z) * 2 + y_hi) * 2 + layer


def everywhere():
    return list(itertools.product(range(4), range(4), range(8), range(2), range(2)))


def pair_route(both):
    route = []
    for x, y_lo, z, y_hi, layer in everywhere():
        to = (x, y_lo ^ 2, z, y_hi, layer)
        if both:
            to = (x, y_lo, z, 1 - y_hi, layer) if layer else (x ^ 1, y_lo, z, y_hi, layer)
        route.append((place(x, y_lo, z, y_hi, layer), place(*to)))
    return route


def groups(both):
    found = {}
    for x, y_lo, z, y_hi, layer in everywhere():
        key = (layer, y_lo // 2, z, y_hi)
        if both:
            key = (layer, x, y_lo, y_hi) if layer else (layer, x % 2, z, y_hi)
        found.setdefault(key, []).append(place(x, y_lo, z, y_hi, layer))
    return sorted(found.values())


def to_pair(piece, both):
    return lax.ppermute(piece, AXES, pair_route(both))


def spread(pairs, both):
    tiles = lax.all_to_all(pairs, AXES, 0, 0, axis_index_groups=groups(both))
    return tiles.reshape((TILES,) + tiles.shape[2:])


def swap(values):
    return lax.ppermute(values, "layer", [(0, 1), (1, 0)])


def per_device(ham_blocks, ham_index, ham_count, dens_blocks, dens_index, dens_count, first_index,
               first_count, second_index, second_count, third_index, third_count):
    index = pltpu.SMEM((2, 1, CAP), jnp.int32)
    packed = pltpu.VMEM((BLK, META), BF)
    payload = call(
        prep_kernel,
        [HBM, SMEM] * 4 + [HBM, HBM],
        (ham_index, ham_count, dens_index, dens_count, first_index, first_count, second_index,
         second_count, ham_blocks, dens_blocks),
        shape(WROWS, LANES),
        [index] * 4 + [packed, packed, pltpu.SemaphoreType.DMA((6,))],
        vmem=62900000,
    )
    half = shape(BT * ROWS, BT * COLS, dtype=F32)
    pairs = call(own_kernel, [VMEM], (payload,), shape(8, 2, WROWS, LANES))
    pairs = call(
        far_kernel, [VMEM] * 2, (to_pair(payload, True), pairs), shape(8, 2, WROWS, LANES),
        alias={1: 0},
    )
    panel = spread(pairs, True)
    dense_ham = shape(BT + 1, BT * ROWS, BT * LANES)
    dense_right = [pltpu.VMEM((BT + 1, BT * COLS, BT * LANES), BF)] * BT
    rounded = pltpu.VMEM((BT * ROWS, BT * COLS), BF)
    code = pltpu.SMEM((TILES, LANES), jnp.int32)
    wire, wires = shape(COLS, WIRE), shape(8, 2, COLS, WIRE)
    note = shape(TILES, LANES, dtype=jnp.int32)
    reading = [pltpu.VMEM((TILES, LANES), jnp.int32), code, pltpu.SemaphoreType.DMA]
    made = (dense_ham,) * BT + (shape(BT + 1, BT * COLS, BT * LANES),) * BT
    *unpacked, own_note = call(local_kernel, [VMEM], (panel,), made + (note,), reading)
    out = call(
        first_kernel,
        [SMEM] * 2 + [VMEM] * 10,
        (first_index, first_count, swap(panel), own_note, *unpacked),
        made + (note, half, wire),
        [pltpu.VMEM((BT * ROWS, BT * COLS), F32), rounded] + reading,
        alias={4 + n: n for n in range(8)},
    )
    ham, (codes, first_term, first_wire) = out[0:4], out[8:]
    dense_half = call(
        dense_kernel, [SMEM, SMEM, VMEM, VMEM], (dens_index, dens_count, dens_blocks, codes), half
    )
    pairs = call(
        lay_kernel,
        [VMEM] * 3,
        (first_wire, to_pair(first_wire, False), dense_half),
        wires,
    )
    real_half, second_wire = call(
        second_kernel,
        [SMEM] * 3 + [VMEM] * 6,
        (codes, second_index, second_count, *ham, spread(pairs, False), dense_half),
        (half, wire),
        dense_right + [rounded],
    )
    pairs = call(
        lay_kernel,
        [VMEM, VMEM, SMEM],
        (second_wire, to_pair(second_wire, False), third_count),
        wires,
    )
    halves = call(
        third_kernel,
        [SMEM] * 3 + [VMEM] * 7,
        (codes, third_index, third_count, *ham, spread(pairs, False), first_term, real_half),
        shape(3 * BT * ROWS, LANES, dtype=F32),
        dense_right,
    )
    whole = shape(SIDE, SIDE, dtype=F32)
    own = call(own_half_kernel, [VMEM], (halves,), (whole, whole))
    return call(other_half_kernel, [VMEM] * 3, (swap(halves), *own), (whole, whole))


def solution(mesh):
    split = Mesh(mesh.devices.reshape(4, 4, 8, 2, 2), AXES)
    row, col = ("x", "y_lo"), ("z", "y_hi")
    blocks, index = P(row, col), P(None, row, col)
    in_specs = (blocks, index, blocks) * 2 + (index, blocks) * 3
    return jax.shard_map(
        per_device, mesh=split, in_specs=in_specs, out_specs=(blocks, blocks), check_vma=False
    )
```

```python
import itertools

import jax
import jax.numpy as jnp
from jax import lax
from jax.experimental import pallas as pl
from jax.experimental.pallas import tpu as pltpu
from jax.sharding import Mesh, PartitionSpec as P

BLK = 92
HALF = 46
BT = 4
CAP = 8
ROWS = 96
COLS = 48
LANES = 128
SIDE = BT * BLK
WIRE = 768
META = 736
CODES = 464
WROWS = WIRE // LANES * BLK
TAIL = WIRE - LANES
TILES = 16
AXES = ("x", "y_lo", "z", "y_hi", "layer")
BF = jnp.bfloat16
F32 = jnp.float32
VMEM = pl.BlockSpec(memory_space=pltpu.VMEM)
SMEM = pl.BlockSpec(memory_space=pltpu.SMEM)
HBM = pl.BlockSpec(memory_space=pltpu.HBM)


def dot_nt(a, b):
    return lax.dot_general(a, b, (((1,), (1,)), ((), ())), preferred_element_type=F32)


def one_hot(shape, shift, width):
    q = lax.broadcasted_iota(jnp.int32, shape, 0)
    x = lax.broadcasted_iota(jnp.int32, shape, 1)
    return jnp.where((x == q + shift) & (q < width), 1.0, 0.0).astype(BF)


def code_of(index_ref, count_ref, s):
    return jnp.where(s < count_ref[0, 0], index_ref[0, 0, s] * BT + index_ref[1, 0, s], -1)


def prep_kernel(hidx_hbm, hcnt_ref, didx_hbm, dcnt_ref, fidx_hbm, fcnt_ref, sidx_hbm, scnt_ref,
                ham_hbm, dens_hbm, out_ref, hidx_ref, didx_ref, fidx_ref, sidx_ref, ham_ref,
                dens_ref, sems):
    pairs = ((ham_hbm, ham_ref), (dens_hbm, dens_ref), (hidx_hbm, hidx_ref), (didx_hbm, didx_ref),
             (fidx_hbm, fidx_ref), (sidx_hbm, sidx_ref))
    copies = [pltpu.make_async_copy(src, dst, sems.at[n]) for n, (src, dst) in enumerate(pairs)]
    for one in copies:
        one.start()
    for one in copies:
        one.wait()
    layer = lax.axis_index("layer")
    lane = lax.broadcasted_iota(jnp.int32, (BLK, LANES), 1) - (META - TAIL)

    def store(wire, *lists):
        tail = wire[:, TAIL:]
        for n, (index_ref, count_ref) in enumerate(lists):
            for s in range(CAP):
                tail = jnp.where(lane == n * CAP + s, code_of(index_ref, count_ref, s).astype(F32), tail)
        for t in range(TAIL // LANES):
            out_ref[t * BLK:(t + 1) * BLK, :] = wire[:, t * LANES:(t + 1) * LANES].astype(BF)
        out_ref[WROWS - BLK:, :] = tail.astype(BF)

    @pl.when(layer == 0)
    def _():
        dens = dens_ref[...]
        pieces = [dot_nt(one_hot((BLK, META), s * BLK, BLK), dens) for s in range(CAP)]
        store(
            jnp.concatenate(pieces + [jnp.zeros((BLK, WIRE - META), F32)], axis=1),
            (didx_ref, dcnt_ref), (fidx_ref, fcnt_ref), (sidx_ref, scnt_ref),
        )

    @pl.when(layer == 1)
    def _():
        wire = jnp.concatenate([ham_ref[...].astype(F32), jnp.zeros((BLK, WIRE - META), F32)], axis=1)
        store(wire, (hidx_ref, hcnt_ref))


def dense_kernel(didx_ref, dcnt_ref, fidx_ref, fcnt_ref, dens_ref, total_ref, dense_ref, first_ref):
    first_ref[...] = keep(all_codes(fidx_ref, fcnt_ref), total_ref[...])
    layer = lax.axis_index("layer")
    dens = dens_ref[...]
    dense_ref[...] = jnp.zeros_like(dense_ref)
    for s in range(CAP):
        code = code_of(didx_ref, dcnt_ref, s)
        at = jnp.maximum(code, 0)
        i, j = at // BT, at % BT
        x = lax.broadcasted_iota(jnp.int32, (META, BT * COLS), 0)
        y = lax.broadcasted_iota(jnp.int32, (META, BT * COLS), 1) - j * COLS
        spread = jnp.where(
            (x == y + (s * BLK + layer * HALF)) & (y >= 0) & (y < HALF) & (code >= 0), 1.0, 0.0
        ).astype(BF)
        block = jnp.dot(dens, spread, preferred_element_type=F32)
        block = jnp.concatenate([block, jnp.zeros((ROWS - BLK, BT * COLS), F32)], axis=0)
        rows = pl.ds(pl.multiple_of(i * ROWS, ROWS), ROWS)
        dense_ref[rows, :] = dense_ref[rows, :] + block


def piece_rows(from_ref, n, first, rows):
    at = [t * BLK + first for t in range(WIRE // LANES)]
    return jnp.concatenate([from_ref[n, row:row + rows, :] for row in at], axis=1)


def unpack_ham(code_ref, g, from_ref, ham_ref):
    for t in range(BT):
        wire = piece_rows(from_ref, g * BT + t, 0, BLK)
        for s in range(CAP):
            code = code_ref[g * BT + t, META - TAIL + s]
            at = jnp.maximum(code, 0)
            where = jnp.where(code >= 0, t, BT)
            rows = pl.ds(pl.multiple_of((at // BT) * ROWS, 16), BLK)
            lanes = pl.ds(pl.multiple_of((at % BT) * LANES, LANES), BLK)
            ham_ref[where, rows, lanes] = wire[:, s * BLK:(s + 1) * BLK]


def unpack_dens(code_ref, g, from_ref, half, right_ref):
    for t, n in enumerate(dens_order(g)):
        wire = piece_rows(from_ref, n, half * HALF, HALF)
        for s in range(CAP):
            code = code_ref[n, META - TAIL + s]
            at = jnp.maximum(code, 0)
            where = jnp.where(code >= 0, t, BT)
            rows = pl.ds(pl.multiple_of((at % BT) * COLS, 16), HALF)
            lanes = pl.ds(pl.multiple_of((at // BT) * LANES, LANES), BLK)
            right_ref[where, rows, lanes] = wire[:, s * BLK:(s + 1) * BLK]


def unpack_right(code_ref, which, wire_ref, order, right_ref, first_row=0):
    for t, n in enumerate(order):
        wire = wire_ref[n, pl.ds(first_row, COLS), :]
        for s in range(CAP):
            code = code_ref[n, META - TAIL + which * CAP + s]
            at = jnp.maximum(code, 0)
            where = jnp.where(code >= 0, t, BT)
            rows = pl.ds(pl.multiple_of((at % BT) * COLS, 16), COLS)
            lanes = pl.ds(pl.multiple_of((at // BT) * LANES, LANES), BLK)
            right_ref[where, rows, lanes] = wire[:, s * BLK:(s + 1) * BLK]


def dens_order(g):
    return [g // 2 * 8 + y_lo * 2 + g % 2 for y_lo in range(BT)]


def term_order(g):
    return [g * BT + y_lo % 2 * 2 + y_lo // 2 for y_lo in range(BT)]


def multiply(total, ham_ref, right_ref):
    for t in range(BT):
        total = total + dot_nt(ham_ref[t], right_ref[t])
    return total


def product(ham_refs, code_ref, which, wire_ref, right_refs):
    total = jnp.zeros((BT * ROWS, BT * COLS), F32)
    right_refs[0][...] = jnp.zeros_like(right_refs[0])
    unpack_right(code_ref, which, wire_ref, term_order(0), right_refs[0])
    for g in range(BT):
        total = multiply(total, ham_refs[g], right_refs[g])
        if g + 1 < BT:
            right_refs[g + 1][...] = jnp.zeros_like(right_refs[g + 1])
            unpack_right(code_ref, which, wire_ref, term_order(g + 1), right_refs[g + 1])
    return total


def keep(codes, total):
    row = lax.broadcasted_iota(jnp.int32, total.shape, 0) // ROWS
    col = lax.broadcasted_iota(jnp.int32, total.shape, 1) // COLS
    place = row * BT + col
    kept = place == codes[0]
    for s in range(1, CAP):
        kept = kept | (place == codes[s])
    return jnp.where(kept, total, 0.0)


def pack(codes, term, rounded_ref, wire_ref):
    rounded_ref[...] = term.astype(BF)
    pieces = []
    for s in range(CAP):
        at = jnp.maximum(codes[s], 0)
        pick = one_hot((COLS, BT * COLS), (at % BT) * COLS, COLS)
        rows = pl.ds(pl.multiple_of((at // BT) * ROWS, 16), ROWS)
        pieces.append(dot_nt(pick, rounded_ref[rows, :]).astype(BF)[:, 0:BLK])
    pieces.append(jnp.zeros((COLS, WIRE - META), BF))
    wire_ref[...] = jnp.concatenate(pieces, axis=1)


def all_codes(index_ref, count_ref):
    return [code_of(index_ref, count_ref, s) for s in range(CAP)]


def read_codes(panel_ref, note_ref, code_ref, sem):
    for k in range(TILES):
        note_ref[k:k + 1, :] = panel_ref[k, CODES:CODES + 16, :][0:1].astype(F32).astype(jnp.int32)
    copy = pltpu.make_async_copy(note_ref, code_ref, sem)
    copy.start()
    copy.wait()


def local_kernel(panel_ref, *refs):
    ham_refs, right_refs, (own_note, note_ref, code_ref, sem) = refs[0:4], refs[4:8], refs[8:]
    layer = lax.axis_index("layer")
    read_codes(panel_ref, note_ref, code_ref, sem)
    own_note[...] = note_ref[...]
    for ref in (*ham_refs, *right_refs):
        ref[...] = jnp.zeros_like(ref)

    @pl.when(layer == 0)
    def _():
        for g in range(BT):
            unpack_dens(code_ref, g, panel_ref, 0, right_refs[g])

    @pl.when(layer == 1)
    def _():
        for g in range(BT):
            unpack_ham(code_ref, g, panel_ref, ham_refs[g])


def first_kernel(index_ref, count_ref, other_ref, own_note, *refs):
    ham_refs, right_refs, (code_out, term_ref, out_ref) = refs[8:12], refs[12:16], refs[16:19]
    total_ref, rounded_ref, note_ref, code_ref, sem = refs[19:]
    layer = lax.axis_index("layer")
    read_codes(other_ref, note_ref, code_ref, sem)
    for g in range(BT):
        for n, to in zip(dens_order(g), term_order(g)):
            code_out[to:to + 1, :] = jnp.where(layer == 0, own_note[n:n + 1, :], note_ref[n:n + 1, :])

    def pipelined(unpack):
        total = jnp.zeros((BT * ROWS, BT * COLS), F32)
        unpack(0)
        for g in range(BT):
            total = multiply(total, ham_refs[g], right_refs[g])
            if g + 1 < BT:
                unpack(g + 1)
        total_ref[...] = total

    @pl.when(layer == 0)
    def _():
        pipelined(lambda g: unpack_ham(code_ref, g, other_ref, ham_refs[g]))

    @pl.when(layer == 1)
    def _():
        pipelined(lambda g: unpack_dens(code_ref, g, other_ref, 1, right_refs[g]))

    codes = all_codes(index_ref, count_ref)
    term_ref[...] = total_ref[...]
    pack(codes, total_ref[...], rounded_ref, out_ref)


def second_kernel(code_ref, index_ref, count_ref, h0, h1, h2, h3, wire_ref, term_ref, out_ref, r0, r1,
                  r2, r3, rounded_ref):
    codes = all_codes(index_ref, count_ref)
    total = product((h0, h1, h2, h3), code_ref, 1, wire_ref, (r0, r1, r2, r3))
    term_ref[...] = total
    pack(codes, total, rounded_ref, out_ref)


def real_kernel(index_ref, count_ref, total_ref, dense_ref, real_ref):
    term = keep(all_codes(index_ref, count_ref), total_ref[...])
    real_ref[...] = dense_ref[...] - 0.5 * term


def third_kernel(code_ref, index_ref, count_ref, h0, h1, h2, h3, wire_ref, first_ref, real_ref,
                 halves_ref, r0, r1, r2, r3):
    codes = all_codes(index_ref, count_ref)
    term = keep(codes, product((h0, h1, h2, h3), code_ref, 2, wire_ref, (r0, r1, r2, r3)))
    rows = BT * ROWS
    real, imag = real_ref[...], term / 6.0 - first_ref[...]
    halves_ref[0:rows] = real[:, 0:LANES]
    halves_ref[rows:2 * rows] = imag[:, 0:LANES]
    halves_ref[2 * rows:3 * rows] = jnp.concatenate([real[:, LANES:], imag[:, LANES:]], axis=1)


def put_half(from_ref, n, layer, out_ref, add):
    rows, rest = BT * ROWS, BT * COLS - LANES
    half = jnp.concatenate(
        [from_ref[n * rows:(n + 1) * rows], from_ref[2 * rows:3 * rows][:, n * rest:(n + 1) * rest]],
        axis=1,
    )
    gap = jnp.zeros((rows, HALF), F32)
    pieces = []
    for j in range(BT):
        piece = half[:, j * COLS:j * COLS + HALF]
        pieces += [gap, piece] if layer else [piece, gap]
    whole = jnp.concatenate(pieces, axis=1)
    for i in range(BT):
        to = slice(i * BLK, (i + 1) * BLK)
        block = whole[i * ROWS:i * ROWS + BLK, :]
        out_ref[to, :] = add[to, :] + block if add is not None else block


def own_half_kernel(own_ref, *out_refs):
    for layer in range(2):
        @pl.when(lax.axis_index("layer") == layer)
        def _(layer=layer):
            for n, out_ref in enumerate(out_refs):
                put_half(own_ref, n, layer, out_ref, None)


def other_half_kernel(other_ref, real_ref, imag_ref, *out_refs):
    for layer in range(2):
        @pl.when(lax.axis_index("layer") == layer)
        def _(layer=layer):
            for n, out_ref in enumerate(out_refs):
                put_half(other_ref, n, 1 - layer, out_ref, (real_ref, imag_ref)[n])


def own_place(by_layer):
    if by_layer:
        return jnp.where(lax.axis_index("layer") == 0, lax.axis_index("x") % 2, lax.axis_index("y_hi"))
    return lax.axis_index("y_lo") // 2


def own_kernel(piece_ref, out_ref):
    at, piece = own_place(True), piece_ref[...]
    for n in range(out_ref.shape[0]):
        out_ref[n, at] = piece


def far_kernel(far_ref, pairs_ref, out_ref):
    del pairs_ref
    at, far = 1 - own_place(True), far_ref[...]
    for n in range(out_ref.shape[0]):
        out_ref[n, at] = far


def lay_kernel(piece_ref, far_ref, *refs):
    out_ref = refs[-1]
    at, piece, far = own_place(False), piece_ref[...], far_ref[...]
    for n in range(out_ref.shape[0]):
        out_ref[n, at] = piece
        out_ref[n, 1 - at] = far


def call(kernel, in_specs, arrays, out_shape, scratch=(), alias=None, vmem=24 << 20):
    return pl.pallas_call(
        kernel,
        out_shape=out_shape,
        in_specs=in_specs,
        out_specs=jax.tree.map(lambda _: VMEM, out_shape),
        input_output_aliases=alias or {},
        scratch_shapes=list(scratch),
        compiler_params=pltpu.CompilerParams(vmem_limit_bytes=vmem),
    )(*arrays)


def shape(*dims, dtype=BF):
    return jax.ShapeDtypeStruct(dims, dtype)


def place(x, y_lo, z, y_hi, layer):
    return (((x * 4 + y_lo) * 8 + z) * 2 + y_hi) * 2 + layer


def everywhere():
    return list(itertools.product(range(4), range(4), range(8), range(2), range(2)))


def pair_route(both):
    route = []
    for x, y_lo, z, y_hi, layer in everywhere():
        to = (x, y_lo ^ 2, z, y_hi, layer)
        if both:
            to = (x, y_lo, z, 1 - y_hi, layer) if layer else (x ^ 1, y_lo, z, y_hi, layer)
        route.append((place(x, y_lo, z, y_hi, layer), place(*to)))
    return route


def groups(both):
    found = {}
    for x, y_lo, z, y_hi, layer in everywhere():
        key = (layer, y_lo // 2, z, y_hi)
        if both:
            key = (layer, x, y_lo, y_hi) if layer else (layer, x % 2, z, y_hi)
        found.setdefault(key, []).append(place(x, y_lo, z, y_hi, layer))
    return sorted(found.values())


def to_pair(piece, both):
    return lax.ppermute(piece, AXES, pair_route(both))


def spread(pairs, both):
    tiles = lax.all_to_all(pairs, AXES, 0, 0, axis_index_groups=groups(both))
    return tiles.reshape((TILES,) + tiles.shape[2:])


def swap(values):
    return lax.ppermute(values, "layer", [(0, 1), (1, 0)])


def per_device(ham_blocks, ham_index, ham_count, dens_blocks, dens_index, dens_count, first_index,
               first_count, second_index, second_count, third_index, third_count):
    index = pltpu.SMEM((2, 1, CAP), jnp.int32)
    packed = pltpu.VMEM((BLK, META), BF)
    payload = call(
        prep_kernel,
        [HBM, SMEM] * 4 + [HBM, HBM],
        (ham_index, ham_count, dens_index, dens_count, first_index, first_count, second_index,
         second_count, ham_blocks, dens_blocks),
        shape(WROWS, LANES),
        [index] * 4 + [packed, packed, pltpu.SemaphoreType.DMA((6,))],
        vmem=62900000,
    )
    half = shape(BT * ROWS, BT * COLS, dtype=F32)
    pairs = call(own_kernel, [VMEM], (payload,), shape(8, 2, WROWS, LANES))
    pairs = call(
        far_kernel, [VMEM] * 2, (to_pair(payload, True), pairs), shape(8, 2, WROWS, LANES),
        alias={1: 0},
    )
    panel = spread(pairs, True)
    dense_ham = shape(BT + 1, BT * ROWS, BT * LANES)
    dense_right = [pltpu.VMEM((BT + 1, BT * COLS, BT * LANES), BF)] * BT
    rounded = pltpu.VMEM((BT * ROWS, BT * COLS), BF)
    code = pltpu.SMEM((TILES, LANES), jnp.int32)
    wire, wires = shape(COLS, WIRE), shape(8, 2, COLS, WIRE)
    note = shape(TILES, LANES, dtype=jnp.int32)
    reading = [pltpu.VMEM((TILES, LANES), jnp.int32), code, pltpu.SemaphoreType.DMA]
    made = (dense_ham,) * BT + (shape(BT + 1, BT * COLS, BT * LANES),) * BT
    *unpacked, own_note = call(local_kernel, [VMEM], (panel,), made + (note,), reading)
    out = call(
        first_kernel,
        [SMEM] * 2 + [VMEM] * 10,
        (first_index, first_count, swap(panel), own_note, *unpacked),
        made + (note, half, wire),
        [pltpu.VMEM((BT * ROWS, BT * COLS), F32), rounded] + reading,
        alias={4 + n: n for n in range(8)},
    )
    ham, (codes, first_total, first_wire) = out[0:4], out[8:]
    dense_half, first_term = call(
        dense_kernel,
        [SMEM] * 4 + [VMEM] * 2,
        (dens_index, dens_count, first_index, first_count, dens_blocks, first_total),
        (half, half),
    )
    pairs = call(
        lay_kernel,
        [VMEM] * 3,
        (first_wire, to_pair(first_wire, False), dense_half),
        wires,
    )
    second_total, second_wire = call(
        second_kernel,
        [SMEM] * 3 + [VMEM] * 5,
        (codes, second_index, second_count, *ham, spread(pairs, False)),
        (half, wire),
        dense_right + [rounded],
    )
    real_half = call(
        real_kernel, [SMEM] * 2 + [VMEM] * 2, (second_index, second_count, second_total, dense_half), half
    )
    pairs = call(
        lay_kernel,
        [VMEM, VMEM, SMEM, VMEM],
        (second_wire, to_pair(second_wire, False), third_count, real_half),
        wires,
    )
    halves = call(
        third_kernel,
        [SMEM] * 3 + [VMEM] * 7,
        (codes, third_index, third_count, *ham, spread(pairs, False), first_term, real_half),
        shape(3 * BT * ROWS, LANES, dtype=F32),
        dense_right,
    )
    whole = shape(SIDE, SIDE, dtype=F32)
    own = call(own_half_kernel, [VMEM], (halves,), (whole, whole))
    return call(other_half_kernel, [VMEM] * 3, (swap(halves), *own), (whole, whole))


def solution(mesh):
    split = Mesh(mesh.devices.reshape(4, 4, 8, 2, 2), AXES)
    row, col = ("x", "y_lo"), ("z", "y_hi")
    blocks, index = P(row, col), P(None, row, col)
    in_specs = (blocks, index, blocks) * 2 + (index, blocks) * 3
    return jax.shard_map(
        per_device, mesh=split, in_specs=in_specs, out_specs=(blocks, blocks), check_vma=False
    )
```

```python
import itertools

import jax
import jax.numpy as jnp
from jax import lax
from jax.experimental import pallas as pl
from jax.experimental.pallas import tpu as pltpu
from jax.sharding import Mesh, PartitionSpec as P

BLK = 92
HALF = 46
BT = 4
CAP = 8
ROWS = 96
COLS = 48
LANES = 128
SIDE = BT * BLK
WIRE = 768
META = 736
CODES = 464
WROWS = WIRE // LANES * BLK
TAIL = WIRE - LANES
TILES = 16
AXES = ("x", "y_lo", "z", "y_hi", "layer")
BF = jnp.bfloat16
F32 = jnp.float32
VMEM = pl.BlockSpec(memory_space=pltpu.VMEM)
SMEM = pl.BlockSpec(memory_space=pltpu.SMEM)
HBM = pl.BlockSpec(memory_space=pltpu.HBM)


def dot_nt(a, b):
    return lax.dot_general(a, b, (((1,), (1,)), ((), ())), preferred_element_type=F32)


def one_hot(shape, shift, width):
    q = lax.broadcasted_iota(jnp.int32, shape, 0)
    x = lax.broadcasted_iota(jnp.int32, shape, 1)
    return jnp.where((x == q + shift) & (q < width), 1.0, 0.0).astype(BF)


def code_of(index_ref, count_ref, s):
    return jnp.where(s < count_ref[0, 0], index_ref[0, 0, s] * BT + index_ref[1, 0, s], -1)


def prep_kernel(hidx_hbm, hcnt_ref, didx_hbm, dcnt_ref, fidx_hbm, fcnt_ref, sidx_hbm, scnt_ref,
                ham_hbm, dens_hbm, out_ref, hidx_ref, didx_ref, fidx_ref, sidx_ref, ham_ref,
                dens_ref, sems):
    def fetch(*pairs):
        copies = [pltpu.make_async_copy(src, dst, sems.at[n]) for n, (src, dst) in enumerate(pairs)]
        for one in copies:
            one.start()
        for one in copies:
            one.wait()

    layer = lax.axis_index("layer")
    lane = lax.broadcasted_iota(jnp.int32, (BLK, LANES), 1) - (META - TAIL)

    def store(wire, *lists):
        tail = wire[:, TAIL:]
        for n, (index_ref, count_ref) in enumerate(lists):
            for s in range(CAP):
                tail = jnp.where(lane == n * CAP + s, code_of(index_ref, count_ref, s).astype(F32), tail)
        for t in range(TAIL // LANES):
            out_ref[t * BLK:(t + 1) * BLK, :] = wire[:, t * LANES:(t + 1) * LANES].astype(BF)
        out_ref[WROWS - BLK:, :] = tail.astype(BF)

    @pl.when(layer == 0)
    def _():
        fetch((dens_hbm, dens_ref), (didx_hbm, didx_ref), (fidx_hbm, fidx_ref), (sidx_hbm, sidx_ref))
        dens = dens_ref[...]
        pieces = [dot_nt(one_hot((BLK, META), s * BLK, BLK), dens) for s in range(CAP)]
        store(
            jnp.concatenate(pieces + [jnp.zeros((BLK, WIRE - META), F32)], axis=1),
            (didx_ref, dcnt_ref), (fidx_ref, fcnt_ref), (sidx_ref, scnt_ref),
        )

    @pl.when(layer == 1)
    def _():
        fetch((ham_hbm, ham_ref), (hidx_hbm, hidx_ref))
        wire = jnp.concatenate([ham_ref[...].astype(F32), jnp.zeros((BLK, WIRE - META), F32)], axis=1)
        store(wire, (hidx_ref, hcnt_ref))


def dense_kernel(didx_ref, dcnt_ref, fidx_ref, fcnt_ref, dens_ref, total_ref, dense_ref, first_ref):
    first_ref[...] = keep(all_codes(fidx_ref, fcnt_ref), total_ref[...])
    layer = lax.axis_index("layer")
    dens = dens_ref[...]
    dense_ref[...] = jnp.zeros_like(dense_ref)
    for s in range(CAP):
        code = code_of(didx_ref, dcnt_ref, s)
        at = jnp.maximum(code, 0)
        i, j = at // BT, at % BT
        x = lax.broadcasted_iota(jnp.int32, (META, BT * COLS), 0)
        y = lax.broadcasted_iota(jnp.int32, (META, BT * COLS), 1) - j * COLS
        spread = jnp.where(
            (x == y + (s * BLK + layer * HALF)) & (y >= 0) & (y < HALF) & (code >= 0), 1.0, 0.0
        ).astype(BF)
        block = jnp.dot(dens, spread, preferred_element_type=F32)
        block = jnp.concatenate([block, jnp.zeros((ROWS - BLK, BT * COLS), F32)], axis=0)
        rows = pl.ds(pl.multiple_of(i * ROWS, ROWS), ROWS)
        dense_ref[rows, :] = dense_ref[rows, :] + block


def piece_rows(from_ref, n, first, rows):
    at = [t * BLK + first for t in range(WIRE // LANES)]
    return jnp.concatenate([from_ref[n, row:row + rows, :] for row in at], axis=1)


def unpack_ham(code_ref, g, from_ref, ham_ref):
    for t in range(BT):
        wire = piece_rows(from_ref, g * BT + t, 0, BLK)
        for s in range(CAP):
            code = code_ref[g * BT + t, META - TAIL + s]
            at = jnp.maximum(code, 0)
            where = jnp.where(code >= 0, t, BT)
            rows = pl.ds(pl.multiple_of((at // BT) * ROWS, 16), BLK)
            lanes = pl.ds(pl.multiple_of((at % BT) * LANES, LANES), BLK)
            ham_ref[where, rows, lanes] = wire[:, s * BLK:(s + 1) * BLK]


def unpack_dens(code_ref, g, from_ref, half, right_ref):
    for t, n in enumerate(dens_order(g)):
        wire = piece_rows(from_ref, n, half * HALF, HALF)
        for s in range(CAP):
            code = code_ref[n, META - TAIL + s]
            at = jnp.maximum(code, 0)
            where = jnp.where(code >= 0, t, BT)
            rows = pl.ds(pl.multiple_of((at % BT) * COLS, 16), HALF)
            lanes = pl.ds(pl.multiple_of((at // BT) * LANES, LANES), BLK)
            right_ref[where, rows, lanes] = wire[:, s * BLK:(s + 1) * BLK]


def unpack_right(code_ref, which, wire_ref, order, right_ref, first_row=0):
    for t, n in enumerate(order):
        wire = wire_ref[n, pl.ds(first_row, COLS), :]
        for s in range(CAP):
            code = code_ref[n, META - TAIL + which * CAP + s]
            at = jnp.maximum(code, 0)
            where = jnp.where(code >= 0, t, BT)
            rows = pl.ds(pl.multiple_of((at % BT) * COLS, 16), COLS)
            lanes = pl.ds(pl.multiple_of((at // BT) * LANES, LANES), BLK)
            right_ref[where, rows, lanes] = wire[:, s * BLK:(s + 1) * BLK]


def dens_order(g):
    return [g // 2 * 8 + y_lo * 2 + g % 2 for y_lo in range(BT)]


def term_order(g):
    return [g * BT + y_lo % 2 * 2 + y_lo // 2 for y_lo in range(BT)]


def multiply(total, ham_ref, right_ref):
    for t in range(BT):
        total = total + dot_nt(ham_ref[t], right_ref[t])
    return total


def product(ham_refs, code_ref, which, wire_ref, right_refs):
    total = jnp.zeros((BT * ROWS, BT * COLS), F32)
    right_refs[0][...] = jnp.zeros_like(right_refs[0])
    unpack_right(code_ref, which, wire_ref, term_order(0), right_refs[0])
    for g in range(BT):
        total = multiply(total, ham_refs[g], right_refs[g])
        if g + 1 < BT:
            right_refs[g + 1][...] = jnp.zeros_like(right_refs[g + 1])
            unpack_right(code_ref, which, wire_ref, term_order(g + 1), right_refs[g + 1])
    return total


def keep(codes, total):
    row = lax.broadcasted_iota(jnp.int32, total.shape, 0) // ROWS
    col = lax.broadcasted_iota(jnp.int32, total.shape, 1) // COLS
    place = row * BT + col
    kept = place == codes[0]
    for s in range(1, CAP):
        kept = kept | (place == codes[s])
    return jnp.where(kept, total, 0.0)


def pack(codes, term, rounded_ref, wire_ref):
    rounded_ref[...] = term.astype(BF)
    pieces = []
    for s in range(CAP):
        at = jnp.maximum(codes[s], 0)
        pick = one_hot((COLS, BT * COLS), (at % BT) * COLS, COLS)
        rows = pl.ds(pl.multiple_of((at // BT) * ROWS, 16), ROWS)
        pieces.append(dot_nt(pick, rounded_ref[rows, :]).astype(BF)[:, 0:BLK])
    pieces.append(jnp.zeros((COLS, WIRE - META), BF))
    wire_ref[...] = jnp.concatenate(pieces, axis=1)


def all_codes(index_ref, count_ref):
    return [code_of(index_ref, count_ref, s) for s in range(CAP)]


def read_codes(panel_ref, note_ref, code_ref, sem):
    for k in range(TILES):
        note_ref[k:k + 1, :] = panel_ref[k, CODES:CODES + 16, :][0:1].astype(F32).astype(jnp.int32)
    copy = pltpu.make_async_copy(note_ref, code_ref, sem)
    copy.start()
    copy.wait()


def local_kernel(panel_ref, *refs):
    ham_refs, right_refs, (own_note, note_ref, code_ref, sem) = refs[0:4], refs[4:8], refs[8:]
    layer = lax.axis_index("layer")
    read_codes(panel_ref, note_ref, code_ref, sem)
    own_note[...] = note_ref[...]
    for ref in (*ham_refs, *right_refs):
        ref[...] = jnp.zeros_like(ref)

    @pl.when(layer == 0)
    def _():
        for g in range(BT):
            unpack_dens(code_ref, g, panel_ref, 0, right_refs[g])

    @pl.when(layer == 1)
    def _():
        for g in range(BT):
            unpack_ham(code_ref, g, panel_ref, ham_refs[g])


def first_kernel(index_ref, count_ref, other_ref, own_note, *refs):
    ham_refs, right_refs, (code_out, term_ref, out_ref) = refs[8:12], refs[12:16], refs[16:19]
    total_ref, rounded_ref, note_ref, code_ref, sem = refs[19:]
    layer = lax.axis_index("layer")
    read_codes(other_ref, note_ref, code_ref, sem)
    for g in range(BT):
        for n, to in zip(dens_order(g), term_order(g)):
            code_out[to:to + 1, :] = jnp.where(layer == 0, own_note[n:n + 1, :], note_ref[n:n + 1, :])

    def pipelined(unpack):
        total = jnp.zeros((BT * ROWS, BT * COLS), F32)
        unpack(0)
        for g in range(BT):
            total = multiply(total, ham_refs[g], right_refs[g])
            if g + 1 < BT:
                unpack(g + 1)
        total_ref[...] = total

    @pl.when(layer == 0)
    def _():
        pipelined(lambda g: unpack_ham(code_ref, g, other_ref, ham_refs[g]))

    @pl.when(layer == 1)
    def _():
        pipelined(lambda g: unpack_dens(code_ref, g, other_ref, 1, right_refs[g]))

    codes = all_codes(index_ref, count_ref)
    term_ref[...] = total_ref[...]
    pack(codes, total_ref[...], rounded_ref, out_ref)


def second_kernel(code_ref, index_ref, count_ref, h0, h1, h2, h3, wire_ref, term_ref, out_ref, r0, r1,
                  r2, r3, rounded_ref):
    codes = all_codes(index_ref, count_ref)
    total = product((h0, h1, h2, h3), code_ref, 1, wire_ref, (r0, r1, r2, r3))
    term_ref[...] = total
    pack(codes, total, rounded_ref, out_ref)


def real_kernel(index_ref, count_ref, total_ref, dense_ref, real_ref):
    term = keep(all_codes(index_ref, count_ref), total_ref[...])
    real_ref[...] = dense_ref[...] - 0.5 * term


def third_kernel(code_ref, index_ref, count_ref, h0, h1, h2, h3, wire_ref, first_ref, real_ref,
                 halves_ref, r0, r1, r2, r3):
    codes = all_codes(index_ref, count_ref)
    term = keep(codes, product((h0, h1, h2, h3), code_ref, 2, wire_ref, (r0, r1, r2, r3)))
    rows = BT * ROWS
    real, imag = real_ref[...], term / 6.0 - first_ref[...]
    halves_ref[0:rows] = real[:, 0:LANES]
    halves_ref[rows:2 * rows] = imag[:, 0:LANES]
    halves_ref[2 * rows:3 * rows] = jnp.concatenate([real[:, LANES:], imag[:, LANES:]], axis=1)


def put_half(from_ref, n, layer, out_ref, add):
    rows, rest = BT * ROWS, BT * COLS - LANES
    half = jnp.concatenate(
        [from_ref[n * rows:(n + 1) * rows], from_ref[2 * rows:3 * rows][:, n * rest:(n + 1) * rest]],
        axis=1,
    )
    gap = jnp.zeros((rows, HALF), F32)
    pieces = []
    for j in range(BT):
        piece = half[:, j * COLS:j * COLS + HALF]
        pieces += [gap, piece] if layer else [piece, gap]
    whole = jnp.concatenate(pieces, axis=1)
    for i in range(BT):
        to = slice(i * BLK, (i + 1) * BLK)
        block = whole[i * ROWS:i * ROWS + BLK, :]
        out_ref[to, :] = add[to, :] + block if add is not None else block


def own_half_kernel(own_ref, *out_refs):
    for layer in range(2):
        @pl.when(lax.axis_index("layer") == layer)
        def _(layer=layer):
            for n, out_ref in enumerate(out_refs):
                put_half(own_ref, n, layer, out_ref, None)


def other_half_kernel(other_ref, real_ref, imag_ref, *out_refs):
    for layer in range(2):
        @pl.when(lax.axis_index("layer") == layer)
        def _(layer=layer):
            for n, out_ref in enumerate(out_refs):
                put_half(other_ref, n, 1 - layer, out_ref, (real_ref, imag_ref)[n])


def own_place(by_layer):
    if by_layer:
        return jnp.where(lax.axis_index("layer") == 0, lax.axis_index("x") % 2, lax.axis_index("y_hi"))
    return lax.axis_index("y_lo") // 2


def own_kernel(piece_ref, out_ref):
    at, piece = own_place(True), piece_ref[...]
    for n in range(out_ref.shape[0]):
        out_ref[n, at] = piece


def far_kernel(far_ref, pairs_ref, out_ref):
    del pairs_ref
    at, far = 1 - own_place(True), far_ref[...]
    for n in range(out_ref.shape[0]):
        out_ref[n, at] = far


def lay_kernel(piece_ref, far_ref, *refs):
    out_ref = refs[-1]
    at, piece, far = own_place(False), piece_ref[...], far_ref[...]
    for n in range(out_ref.shape[0]):
        out_ref[n, at] = piece
        out_ref[n, 1 - at] = far


def call(kernel, in_specs, arrays, out_shape, scratch=(), alias=None, vmem=24 << 20):
    return pl.pallas_call(
        kernel,
        out_shape=out_shape,
        in_specs=in_specs,
        out_specs=jax.tree.map(lambda _: VMEM, out_shape),
        input_output_aliases=alias or {},
        scratch_shapes=list(scratch),
        compiler_params=pltpu.CompilerParams(vmem_limit_bytes=vmem),
    )(*arrays)


def shape(*dims, dtype=BF):
    return jax.ShapeDtypeStruct(dims, dtype)


def place(x, y_lo, z, y_hi, layer):
    return (((x * 4 + y_lo) * 8 + z) * 2 + y_hi) * 2 + layer


def everywhere():
    return list(itertools.product(range(4), range(4), range(8), range(2), range(2)))


def pair_route(both):
    route = []
    for x, y_lo, z, y_hi, layer in everywhere():
        to = (x, y_lo ^ 2, z, y_hi, layer)
        if both:
            to = (x, y_lo, z, 1 - y_hi, layer) if layer else (x ^ 1, y_lo, z, y_hi, layer)
        route.append((place(x, y_lo, z, y_hi, layer), place(*to)))
    return route


def groups(both):
    found = {}
    for x, y_lo, z, y_hi, layer in everywhere():
        key = (layer, y_lo // 2, z, y_hi)
        if both:
            key = (layer, x, y_lo, y_hi) if layer else (layer, x % 2, z, y_hi)
        found.setdefault(key, []).append(place(x, y_lo, z, y_hi, layer))
    return sorted(found.values())


def to_pair(piece, both):
    return lax.ppermute(piece, AXES, pair_route(both))


def spread(pairs, both):
    tiles = lax.all_to_all(pairs, AXES, 0, 0, axis_index_groups=groups(both))
    return tiles.reshape((TILES,) + tiles.shape[2:])


def swap(values):
    return lax.ppermute(values, "layer", [(0, 1), (1, 0)])


def per_device(ham_blocks, ham_index, ham_count, dens_blocks, dens_index, dens_count, first_index,
               first_count, second_index, second_count, third_index, third_count):
    index = pltpu.SMEM((2, 1, CAP), jnp.int32)
    packed = pltpu.VMEM((BLK, META), BF)
    payload = call(
        prep_kernel,
        [HBM, SMEM] * 4 + [HBM, HBM],
        (ham_index, ham_count, dens_index, dens_count, first_index, first_count, second_index,
         second_count, ham_blocks, dens_blocks),
        shape(WROWS, LANES),
        [index] * 4 + [packed, packed, pltpu.SemaphoreType.DMA((4,))],
        vmem=62900000,
    )
    half = shape(BT * ROWS, BT * COLS, dtype=F32)
    pairs = call(own_kernel, [VMEM], (payload,), shape(8, 2, WROWS, LANES))
    pairs = call(
        far_kernel, [VMEM] * 2, (to_pair(payload, True), pairs), shape(8, 2, WROWS, LANES),
        alias={1: 0},
    )
    panel = spread(pairs, True)
    dense_ham = shape(BT + 1, BT * ROWS, BT * LANES)
    dense_right = [pltpu.VMEM((BT + 1, BT * COLS, BT * LANES), BF)] * BT
    rounded = pltpu.VMEM((BT * ROWS, BT * COLS), BF)
    code = pltpu.SMEM((TILES, LANES), jnp.int32)
    wire, wires = shape(COLS, WIRE), shape(8, 2, COLS, WIRE)
    note = shape(TILES, LANES, dtype=jnp.int32)
    reading = [pltpu.VMEM((TILES, LANES), jnp.int32), code, pltpu.SemaphoreType.DMA]
    made = (dense_ham,) * BT + (shape(BT + 1, BT * COLS, BT * LANES),) * BT
    *unpacked, own_note = call(local_kernel, [VMEM], (panel,), made + (note,), reading)
    out = call(
        first_kernel,
        [SMEM] * 2 + [VMEM] * 10,
        (first_index, first_count, swap(panel), own_note, *unpacked),
        made + (note, half, wire),
        [pltpu.VMEM((BT * ROWS, BT * COLS), F32), rounded] + reading,
        alias={4 + n: n for n in range(8)},
    )
    ham, (codes, first_total, first_wire) = out[0:4], out[8:]
    dense_half, first_term = call(
        dense_kernel,
        [SMEM] * 4 + [VMEM] * 2,
        (dens_index, dens_count, first_index, first_count, dens_blocks, first_total),
        (half, half),
    )
    pairs = call(
        lay_kernel,
        [VMEM] * 3,
        (first_wire, to_pair(first_wire, False), dense_half),
        wires,
    )
    second_total, second_wire = call(
        second_kernel,
        [SMEM] * 3 + [VMEM] * 5,
        (codes, second_index, second_count, *ham, spread(pairs, False)),
        (half, wire),
        dense_right + [rounded],
    )
    real_half = call(
        real_kernel, [SMEM] * 2 + [VMEM] * 2, (second_index, second_count, second_total, dense_half), half
    )
    pairs = call(
        lay_kernel,
        [VMEM, VMEM, SMEM, VMEM],
        (second_wire, to_pair(second_wire, False), third_count, real_half),
        wires,
    )
    halves = call(
        third_kernel,
        [SMEM] * 3 + [VMEM] * 7,
        (codes, third_index, third_count, *ham, spread(pairs, False), first_term, real_half),
        shape(3 * BT * ROWS, LANES, dtype=F32),
        dense_right,
    )
    whole = shape(SIDE, SIDE, dtype=F32)
    own = call(own_half_kernel, [VMEM], (halves,), (whole, whole))
    return call(other_half_kernel, [VMEM] * 3, (swap(halves), *own), (whole, whole))


def solution(mesh):
    split = Mesh(mesh.devices.reshape(4, 4, 8, 2, 2), AXES)
    row, col = ("x", "y_lo"), ("z", "y_hi")
    blocks, index = P(row, col), P(None, row, col)
    in_specs = (blocks, index, blocks) * 2 + (index, blocks) * 3
    return jax.shard_map(
        per_device, mesh=split, in_specs=in_specs, out_specs=(blocks, blocks), check_vma=False
    )
```
